32 devices in a mesh: slab: 2 (over x), energy: 16 (over z, y, core).
Axes of the slice: x: 2, y: 2, z: 4, core: 2. Of those that a mesh axis runs over, the one named last changes fastest.
Arguments:
- retarded: bfloat16 [32, 3, 384, 384], P('energy', None, 'slab'), may hold values from -0.3125 to 0.3125
- injection: bfloat16 [32, 2, 384, 384], P('energy', None, 'slab'), may hold values from -6 to 6
- screened: bfloat16 [32, 2, 384, 384], P('energy', None, 'slab'), may hold values from -6 to 6
- pattern: int32 [384], P('slab'), may hold values from 0 to 1, as said below
Outputs:
- self_energy: bfloat16 [32, 2, 384, 384], P('energy', None, 'slab')
The draws below stay inside these ranges and needn't reach their ends.
Inputs may be any that keep to these rules, and one draw needn't show every extreme that they name: `pattern`: exactly 128 of the 192 entries held by each index of slab are 1.
All inputs are finite; a program needn't handle non-finite values.
Results may differ from the reference program's by a relative error of at most 0.0058.
Values may be sent and summed in bfloat16 or wider, within the bound.
A program may use at most 64 MiB of HBM per device.

```python
import math
import jax
import jax.numpy as jnp
from jax import lax

B = 192
SB = 1
ENERGIES = 32
NS = 2
ROWS = 384
LIVE = 128


def draw_pattern(key, part):
    groups = NS // SB
    per_device = SB * B
    group_keys = jax.random.split(jax.random.fold_in(key, 17), groups)

    def one_group(group_key):
        shuffled = jax.random.permutation(group_key, per_device)
        return (shuffled < LIVE).astype(jnp.int32)
    return jax.vmap(one_group)(group_keys).reshape(NS * B)


def block_levels(stream_key, shape, cuts, least, top_value):
    factor_of, own = 1.0, jax.random.fold_in(stream_key, 6)
    for axis_at, blocks in cuts:
        draws = jnp.exp(jax.random.uniform(jax.random.fold_in(own, axis_at), (blocks,), jnp.float32, least / len(cuts), top_value / len(cuts)))
        factor_of = factor_of * jnp.repeat(draws, shape[axis_at] // blocks).reshape([-1 if axis == axis_at else 1 for axis in range(len(shape))])
    return factor_of


def centred(key, shape, scale, most, shards=(), kind=jnp.bfloat16):
    level = block_levels(key, shape, shards, -0.22, 0.18) if shards else 1.0
    entries = jax.random.normal(key, shape, jnp.float32) * scale * level
    return jnp.minimum(jnp.maximum(entries, -most), most).astype(kind)


def setup_inputs(seed: int = 0) -> dict:
    keys = jax.random.split(jax.random.key(seed), 5)
    return {
        "retarded": centred(keys[0], (ENERGIES, 3, ROWS, 2 * B), (2 * B) ** -0.5, 0.3125, ((0, 16), (2, 2))),
        "injection": centred(keys[1], (ENERGIES, 2, ROWS, 2 * B), 1.0, 6.0, ((0, 16), (2, 2))),
        "screened": centred(keys[2], (ENERGIES, 2, ROWS, 2 * B), 1.0, 6.0, ((0, 16), (2, 2))),
        "pattern": draw_pattern(jax.random.fold_in(keys[4], 71), 0),
    }


def stack_complex(blocks):
    half = blocks.shape[-1] // 2
    real_part = blocks[..., :half]
    imag_part = blocks[..., half:]
    upper = jnp.concatenate([real_part, imag_part], -1)
    lower = jnp.concatenate([-imag_part, real_part], -1)
    return jnp.concatenate([upper, lower], -2)

def convolve(green, screen):
    count = green.shape[0]
    half = green.shape[-1] // 2
    energy_index = jnp.arange(count, dtype=jnp.int32)
    phase_angle = 2.0 * math.pi / count * (energy_index[:, None] * energy_index[None, :] % count).astype(jnp.float32)
    cosine_table = jnp.cos(phase_angle)
    sine_table = jnp.sin(phase_angle)

    def transform(values):
        flat = values.reshape(count, -1)
        with_cos = jnp.dot(cosine_table, flat, precision=lax.Precision.HIGHEST).reshape(values.shape)
        with_sin = jnp.dot(sine_table, flat, precision=lax.Precision.HIGHEST).reshape(values.shape)
        return (with_cos, with_sin)

    def forward(values):
        with_cos, with_sin = transform(values.astype(jnp.float32))
        return (with_cos[..., :half] + with_sin[..., half:], with_cos[..., half:] - with_sin[..., :half])
    green_real, green_imag = forward(green)
    screen_real, screen_imag = forward(screen)
    prod_real = green_real * screen_real - green_imag * screen_imag
    prod_imag = green_real * screen_imag + green_imag * screen_real
    with_cos, with_sin = transform(jnp.concatenate([prod_real, prod_imag], -1))
    sigma_real = with_cos[..., :half] - with_sin[..., half:]
    sigma_imag = with_cos[..., half:] + with_sin[..., :half]
    factor = 1.0 / (count * math.sqrt(count))
    return jnp.concatenate([-sigma_imag, sigma_real], -1) * factor

def triple(rows_energy, inject_energy):
    zero_block = jnp.zeros((2, 1, B, 2 * B), inject_energy.dtype)
    padded = jnp.concatenate([zero_block, inject_energy, zero_block], 1)
    total = jnp.zeros((2, NS, B, 2 * B), jnp.float32)
    for offset in range(3):
        nearby = padded[:, offset:offset + NS]
        expanded = stack_complex(nearby).astype(jnp.float32)
        row_block = rows_energy[offset].astype(jnp.float32)
        left_product = jnp.einsum('nac,lncd->lnad', row_block, expanded).astype(jnp.bfloat16)
        left_product = lax.optimization_barrier(left_product)
        left_wide = left_product.astype(jnp.float32)
        swapped = jnp.concatenate([left_wide[..., B:], -left_wide[..., :B]], -1)
        real_part = jnp.einsum('lnac,nbc->lnab', left_wide, row_block)
        imag_part = jnp.einsum('lnac,nbc->lnab', swapped, row_block)
        total = total + jnp.concatenate([real_part, imag_part], -1)
    return total.astype(jnp.bfloat16)

def reference(retarded, injection, screened, pattern):
    rows_all = retarded.reshape(ENERGIES, 3, NS, B, 2 * B)
    inject_all = injection.reshape(ENERGIES, 2, NS, B, 2 * B)
    screen_all = screened.reshape(ENERGIES, 2, NS, B, 2 * B)

    def one_energy(pair):
        return triple(pair[0], pair[1])
    green = lax.map(one_energy, (rows_all, inject_all))

    def one_block(index):
        green_block = lax.dynamic_index_in_dim(green, index, 2, keepdims=False)
        screen_block = lax.dynamic_index_in_dim(screen_all, index, 2, keepdims=False)
        return convolve(green_block, screen_block)
    sigma = lax.map(one_block, jnp.arange(NS, dtype=jnp.int32))
    sigma = jnp.moveaxis(sigma, 0, 2).reshape(ENERGIES, 2, ROWS, 2 * B)
    sigma = sigma * pattern.astype(jnp.float32)[None, None, :, None]
    return sigma.astype(jnp.bfloat16)
```

```python
import functools
import math

import jax
import jax.numpy as jnp
import numpy as np
from jax import lax
from jax.experimental import pallas as pl
from jax.experimental.pallas import tpu as pltpu
from jax.sharding import PartitionSpec as P

MESH = pl.DeviceIdType.MESH
F32 = jnp.float32
BF16 = jnp.bfloat16


def dot(a, b):
    return jnp.dot(a, b, preferred_element_type=F32)


def dot_nt(a, b):
    return lax.dot_general(a, b, (((1,), (1,)), ((), ())), preferred_element_type=F32)


def times_i(x):
    half = x.shape[-1] // 2
    lane = lax.broadcasted_iota(jnp.int32, x.shape, 1)
    turned = pltpu.roll(x, half, 1)
    return jnp.where(lane < half, -turned, turned)


def complex_times(x, y):
    half = x.shape[-1] // 2
    first = lax.broadcasted_iota(jnp.int32, x.shape, 1) < half
    turned = pltpu.roll(y, half, 1)
    return x * jnp.where(first, y, turned) + times_i(x) * jnp.where(first, turned, y)


def kernel(
    retarded, injection, screened, pattern, tables, want_slot, want_col, want_row,
    result,
    ret_v, inj_v, scr_v, tab_v, halo, row_wide, row_live, total, screen_hat, out_v,
    s_send, s_recv, g_send, g_recv, c_send, c_recv,
    load_sem, halo_out, halo_in, s_out, s_in, g_out, g_in, c_out, c_in, store_sem,
):
    owners = lax.axis_size("energy")
    slabs = lax.axis_size("slab")
    me = lax.axis_index("energy")
    slab = lax.axis_index("slab")
    has_left = slab > 0
    has_right = slab < slabs - 1
    energies, _, block, width = ret_v.shape
    chunk = s_send.shape[2]
    per_energy = chunk // energies
    flat = owners * chunk
    count = owners * energies

    loads = [
        pltpu.make_async_copy(source, target, load_sem.at[at])
        for at, (source, target) in enumerate(
            [(screened, scr_v), (retarded, ret_v), (injection, inj_v), (tables, tab_v)]
        )
    ]
    for load in loads:
        load.start()

    barrier = pltpu.get_barrier_semaphore()

    def greet(step, carry):
        peer = lax.rem(me + step, owners)
        pl.semaphore_signal(barrier, inc=1, device_id={"energy": peer}, device_id_type=MESH)
        return carry

    lax.fori_loop(1, owners, greet, 0)

    @pl.when(has_left)
    def _():
        pl.semaphore_signal(barrier, inc=1, device_id={"slab": slab - 1}, device_id_type=MESH)

    @pl.when(has_right)
    def _():
        pl.semaphore_signal(barrier, inc=1, device_id={"slab": slab + 1}, device_id_type=MESH)

    pl.semaphore_wait(
        barrier, owners - 1 + has_left.astype(jnp.int32) + has_right.astype(jnp.int32)
    )

    def halo_copy(side, kind):
        return pltpu.make_async_remote_copy(
            src_ref=injection.at[:, kind],
            dst_ref=halo.at[side, kind],
            send_sem=halo_out.at[side, kind],
            recv_sem=halo_in.at[side, kind],
            device_id={"slab": slab + 1 - 2 * side},
            device_id_type=MESH,
        )

    for kind in range(2):
        @pl.when(has_right)
        def _():
            halo_copy(0, kind).start()

        @pl.when(has_left)
        def _():
            halo_copy(1, kind).start()

    def spread(source, target, out_sem, in_sem):
        def send(step, carry):
            peer = lax.rem(me + step, owners)
            pltpu.make_async_remote_copy(
                src_ref=source.at[peer],
                dst_ref=target.at[me],
                send_sem=out_sem,
                recv_sem=in_sem,
                device_id={"energy": peer},
                device_id_type=MESH,
            ).start()
            return carry

        lax.fori_loop(1, owners, send, 0)
        target[me] = source[me]

    def wait_all(buffer, sem):
        rest = buffer.at[pl.ds(0, owners - 1)]
        pltpu.make_async_copy(rest, rest, sem).wait()

    pattern_row = pattern[...].astype(F32)
    down = lax.broadcasted_iota(jnp.int32, (block, block), 0)
    across = lax.broadcasted_iota(jnp.int32, (block, block), 1)
    pattern_col = jnp.sum(jnp.where(down == across, pattern_row, 0.0), 1, keepdims=True)
    rank_col = jnp.sum(jnp.where(across < down, pattern_row, 0.0), 1, keepdims=True)
    rank_row = jnp.sum(jnp.where(down < across, pattern_col, 0.0), 0, keepdims=True)
    key_col = jnp.where(pattern_col > 0.5, rank_col, -1.0)
    key_row = jnp.where(pattern_row > 0.5, rank_row, -1.0)

    def one_hot(left, right):
        return jnp.where(left == right, 1.0, 0.0).astype(BF16)

    loads[0].wait()
    picks = [one_hot(want_col[e], key_row) for e in range(energies)]
    for kind in range(2):
        picked = sum(dot(picks[e], scr_v[e, kind]) for e in range(energies))
        s_send[:, kind] = picked.astype(BF16).reshape(owners, chunk, width)
    spread(s_send, s_recv, s_out, s_in)

    pick_rows = one_hot(want_slot[...], key_row)

    def widen(x):
        return times_i(x.astype(F32)).astype(BF16)

    def prepare(offset):
        for e in range(energies):
            rows = ret_v[e, offset]
            row_wide[offset, e, :block] = rows
            row_wide[offset, e, block:] = widen(rows)
            row_live[offset, e] = dot(pick_rows, rows).astype(BF16)

    def term(offset, e, inject):
        expanded = jnp.concatenate([inject, widen(inject)], 0)
        left = dot(row_live[offset, e], expanded).astype(BF16)
        return dot_nt(left, row_wide[offset, e])

    loads[1].wait()
    loads[2].wait()
    prepare(1)

    @pl.when(has_left)
    def _():
        prepare(0)

    @pl.when(has_right)
    def _():
        prepare(2)

    for kind in range(2):
        for e in range(energies):
            total[kind, e] = term(1, e, inj_v[e, kind])

    def green(kind):
        @pl.when(has_left)
        def _():
            halo_copy(0, kind).wait_recv()
            for e in range(energies):
                total[kind, e] += term(0, e, halo[0, kind, e])

        @pl.when(has_right)
        def _():
            halo_copy(1, kind).wait_recv()
            for e in range(energies):
                total[kind, e] += term(2, e, halo[1, kind, e])

        parts = [total[kind, e].reshape(owners, per_energy, width) for e in range(energies)]
        g_send[kind] = jnp.concatenate(parts, 1).astype(BF16)
        spread(g_send.at[kind], g_recv.at[kind], g_out.at[kind], g_in.at[kind])

    def forward(values):
        with_cos = dot(tab_v[0], values) + dot(tab_v[2], values)
        with_sin = dot(tab_v[1], values) + dot(tab_v[3], values)
        return with_cos - times_i(with_sin)

    factor = 1.0 / (count * math.sqrt(count))

    def convolve(kind):
        wait_all(g_recv.at[kind], g_in.at[kind])
        green_hat = forward(g_recv[kind].reshape(flat, width))
        product = complex_times(green_hat, screen_hat[kind])
        high = product.astype(BF16)
        low = (product - high.astype(F32)).astype(BF16)
        with_cos = dot(tab_v[0], high) + dot(tab_v[2], high) + dot(tab_v[0], low)
        with_sin = dot(tab_v[1], high) + dot(tab_v[3], high) + dot(tab_v[1], low)
        sigma = (times_i(with_cos) - with_sin) * factor
        c_send[kind] = sigma.astype(BF16).reshape(owners, chunk, width)
        spread(c_send.at[kind], c_recv.at[kind], c_out.at[kind], c_in.at[kind])

    green(0)
    loads[3].wait()
    wait_all(s_recv, s_in)
    for kind in range(2):
        screen_hat[kind] = forward(s_recv[:, kind].reshape(flat, width))
    green(1)
    convolve(0)
    convolve(1)

    places = [one_hot(key_col, want_row[e]) for e in range(energies)]
    stores = []
    for kind in range(2):
        wait_all(c_recv.at[kind], c_in.at[kind])
        back = c_recv[kind].reshape(flat, width)
        for e in range(energies):
            out_v[kind, e] = dot(places[e], back).astype(BF16)
        store = pltpu.make_async_copy(out_v.at[kind], result.at[:, kind], store_sem.at[kind])
        store.start()
        stores.append(store)

    for kind in range(2):
        @pl.when(has_right)
        def _():
            halo_copy(0, kind).wait_send()

        @pl.when(has_left)
        def _():
            halo_copy(1, kind).wait_send()

    wait_all(s_send, s_out)
    for kind in range(2):
        wait_all(g_send.at[kind], g_out.at[kind])
        wait_all(c_send.at[kind], c_out.at[kind])
        stores[kind].wait()


def layout(owners, energies, live):
    share = -(-live // owners)
    padded = -(-share // 8) * 8
    while energies * padded % 16:
        padded += 8
    slot = np.arange(owners * padded)
    wanted = slot // padded * share + slot % padded
    wanted = np.where((slot % padded < share) & (wanted < live), wanted, -2)
    by_energy = np.full((energies, owners, energies, padded), -2)
    for e in range(energies):
        by_energy[e, :, e] = wanted.reshape(owners, padded)
    by_energy = by_energy.reshape(energies, -1)
    count = owners * energies
    index = np.arange(count)
    angle = 2.0 * np.pi / count * (index[:, None] * index[None, :] % count)
    tables = np.stack([np.cos(angle), np.sin(angle)]).astype(np.float32)
    high = tables.astype(jnp.bfloat16)
    low = (tables - high.astype(np.float32)).astype(jnp.bfloat16)
    small = np.concatenate([high, low]).astype(np.float32)
    eye = np.eye(padded, dtype=np.float32)
    wide = np.stack([np.kron(table, eye) for table in small]).astype(jnp.bfloat16)
    return padded, wanted.astype(np.float32), by_energy.astype(np.float32), wide


def local(retarded, injection, screened, pattern):
    energies, _, block, width = retarded.shape
    owners = lax.axis_size("energy")
    live = block * 2 // 3
    padded, wanted, by_energy, tables = layout(owners, energies, live)
    chunk = energies * padded
    flat = owners * chunk
    slots = owners * padded
    anywhere = pl.BlockSpec(memory_space=pl.ANY)
    vmem = pl.BlockSpec(memory_space=pltpu.VMEM)
    dma = pltpu.SemaphoreType.DMA
    blocks = (2, owners, chunk, width)
    return pl.pallas_call(
        kernel,
        out_shape=jax.ShapeDtypeStruct(screened.shape, BF16),
        in_specs=[anywhere] * 3 + [vmem, anywhere] + [vmem] * 3,
        out_specs=anywhere,
        scratch_shapes=[
            pltpu.VMEM(retarded.shape, BF16),
            pltpu.VMEM(injection.shape, BF16),
            pltpu.VMEM(screened.shape, BF16),
            pltpu.VMEM(tables.shape, BF16),
            pltpu.VMEM((2, 2, energies, block, width), BF16),
            pltpu.VMEM((3, energies, 2 * block, width), BF16),
            pltpu.VMEM((3, energies, slots, width), BF16),
            pltpu.VMEM((2, energies, slots, width), F32),
            pltpu.VMEM((2, flat, width), F32),
            pltpu.VMEM((2, energies, block, width), BF16),
            pltpu.VMEM((owners, 2, chunk, width), BF16),
            pltpu.VMEM((owners, 2, chunk, width), BF16),
            pltpu.VMEM(blocks, BF16),
            pltpu.VMEM(blocks, BF16),
            pltpu.VMEM(blocks, BF16),
            pltpu.VMEM(blocks, BF16),
            dma((4,)),
            dma((2, 2)),
            dma((2, 2)),
            dma,
            dma,
            dma((2,)),
            dma((2,)),
            dma((2,)),
            dma((2,)),
            dma((2,)),
        ],
        compiler_params=pltpu.CompilerParams(
            collective_id=0, has_side_effects=True, vmem_limit_bytes=56 * 1024 * 1024
        ),
    )(
        retarded,
        injection,
        screened,
        pattern.reshape(1, -1),
        jnp.asarray(tables),
        jnp.asarray(wanted.reshape(-1, 1)),
        jnp.asarray(by_energy.reshape(energies, -1, 1)),
        jnp.asarray(by_energy.reshape(energies, 1, -1)),
    )


def solution(mesh):
    placed = (
        P("energy", None, "slab", None),
        P("energy", None, "slab", None),
        P("energy", None, "slab", None),
        P("slab"),
    )
    return jax.shard_map(
        local,
        mesh=mesh,
        in_specs=placed,
        out_specs=P("energy", None, "slab", None),
        check_vma=False,
    )
```

```python
import math

import jax
import jax.numpy as jnp
import numpy as np
from jax import lax
from jax.experimental import pallas as pl
from jax.experimental.pallas import tpu as pltpu
from jax.sharding import PartitionSpec as P

MESH = pl.DeviceIdType.MESH
F32 = jnp.float32
BF16 = jnp.bfloat16


def dot(a, b):
    return jnp.dot(a, b, preferred_element_type=F32)


def dot_nt(a, b):
    return lax.dot_general(a, b, (((1,), (1,)), ((), ())), preferred_element_type=F32)


def times_i(x):
    half = x.shape[-1] // 2
    lane = lax.broadcasted_iota(jnp.int32, x.shape, 1)
    turned = pltpu.roll(x, half, 1)
    return jnp.where(lane < half, -turned, turned)


def complex_times(x, y):
    half = x.shape[-1] // 2
    first = lax.broadcasted_iota(jnp.int32, x.shape, 1) < half
    turned = pltpu.roll(y, half, 1)
    return x * jnp.where(first, y, turned) + times_i(x) * jnp.where(first, turned, y)


def kernel(
    retarded, injection, screened, pattern, tables, want_slot, want_col, want_row,
    back, places,
    ret_v, inj_v, scr_v, pat_v, tab_v, slot_v, col_v, row_v,
    halo, row_wide, row_live, total, screen_hat,
    places_v, s_send, s_recv, g_send, g_recv, c_send,
    load_sem, halo_out, halo_in, s_out, s_in, g_out, g_in, c_out, c_in, own_sem, store_sem,
):
    owners = lax.axis_size("energy")
    slabs = lax.axis_size("slab")
    me = lax.axis_index("energy")
    slab = lax.axis_index("slab")
    has_left = slab > 0
    has_right = slab < slabs - 1
    energies, _, block, width = ret_v.shape
    chunk = s_send.shape[2]
    per_energy = chunk // energies
    flat = owners * chunk
    count = owners * energies

    loads = [
        pltpu.make_async_copy(source, target, load_sem.at[at])
        for at, (source, target) in enumerate(
            [
                (pattern, pat_v),
                (want_col, col_v),
                (screened, scr_v),
                (want_slot, slot_v),
                (retarded, ret_v),
                (injection, inj_v),
                (tables, tab_v),
                (want_row, row_v),
            ]
        )
    ]
    for load in loads:
        load.start()

    barrier = pltpu.get_barrier_semaphore()

    def greet(step, carry):
        peer = lax.rem(me + step, owners)
        pl.semaphore_signal(barrier, inc=1, device_id={"energy": peer}, device_id_type=MESH)
        return carry

    lax.fori_loop(1, owners, greet, 0)

    @pl.when(has_left)
    def _():
        pl.semaphore_signal(barrier, inc=1, device_id={"slab": slab - 1}, device_id_type=MESH)

    @pl.when(has_right)
    def _():
        pl.semaphore_signal(barrier, inc=1, device_id={"slab": slab + 1}, device_id_type=MESH)

    def spread(source, target, out_sem, in_sem):
        half = owners // 2
        while half:
            group = me // half
            first = (group + 1 - 2 * lax.rem(group, 2)) * half

            def send(step, carry, half=half, first=first):
                peer = first + lax.rem(me + step, half)
                pltpu.make_async_remote_copy(
                    src_ref=source.at[peer],
                    dst_ref=target.at[me],
                    send_sem=out_sem,
                    recv_sem=in_sem,
                    device_id={"energy": peer},
                    device_id_type=MESH,
                ).start()
                return carry

            lax.fori_loop(0, half, send, 0)
            half //= 2

    def wait_all(buffer, sem):
        rest = buffer.at[pl.ds(0, owners - 1)]
        pltpu.make_async_copy(rest, rest, sem).wait()

    loads[0].wait()
    pattern_row = pat_v[...].astype(F32)
    down = lax.broadcasted_iota(jnp.int32, (block, block), 0)
    across = lax.broadcasted_iota(jnp.int32, (block, block), 1)
    pattern_col = jnp.sum(jnp.where(down == across, pattern_row, 0.0), 1, keepdims=True)
    rank_col = jnp.sum(jnp.where(across < down, pattern_row, 0.0), 1, keepdims=True)
    rank_row = jnp.sum(jnp.where(down < across, pattern_col, 0.0), 0, keepdims=True)
    key_col = jnp.where(pattern_col > 0.5, rank_col, -1.0)
    key_row = jnp.where(pattern_row > 0.5, rank_row, -1.0)

    def one_hot(left, right):
        return jnp.where(left == right, 1.0, 0.0).astype(BF16)

    loads[1].wait()
    picks = [one_hot(col_v[e], key_row) for e in range(energies)]
    loads[2].wait()
    for kind in range(2):
        picked = sum(dot(picks[e], scr_v[e, kind]) for e in range(energies))
        s_send[:, kind] = picked.astype(BF16).reshape(owners, chunk, width)

    pl.semaphore_wait(
        barrier, owners - 1 + has_left.astype(jnp.int32) + has_right.astype(jnp.int32)
    )

    def halo_copy(side, kind):
        return pltpu.make_async_remote_copy(
            src_ref=injection.at[:, kind],
            dst_ref=halo.at[side, kind],
            send_sem=halo_out.at[side, kind],
            recv_sem=halo_in.at[side, kind],
            device_id={"slab": slab + 1 - 2 * side},
            device_id_type=MESH,
        )

    for kind in range(2):
        @pl.when(has_right)
        def _():
            halo_copy(0, kind).start()

        @pl.when(has_left)
        def _():
            halo_copy(1, kind).start()

    spread(s_send, s_recv, s_out, s_in)
    s_recv[me] = s_send[me]

    loads[3].wait()
    pick_rows = one_hot(slot_v[...], key_row)

    def widen(x):
        return times_i(x.astype(F32)).astype(BF16)

    def prepare(offset):
        for e in range(energies):
            rows = ret_v[e, offset]
            row_wide[offset, e, :block] = rows
            row_wide[offset, e, block:] = widen(rows)
            row_live[offset, e] = dot(pick_rows, rows).astype(BF16)

    def term(offset, e, inject):
        expanded = jnp.concatenate([inject, widen(inject)], 0)
        left = dot(row_live[offset, e], expanded).astype(BF16)
        return dot_nt(left, row_wide[offset, e])

    loads[4].wait()
    loads[5].wait()
    prepare(1)

    @pl.when(has_left)
    def _():
        prepare(0)

    @pl.when(has_right)
    def _():
        prepare(2)

    for kind in range(2):
        for e in range(energies):
            total[kind, e] = term(1, e, inj_v[e, kind])

    def green(kind):
        @pl.when(has_left)
        def _():
            halo_copy(0, kind).wait_recv()
            for e in range(energies):
                total[kind, e] += term(0, e, halo[0, kind, e])

        @pl.when(has_right)
        def _():
            halo_copy(1, kind).wait_recv()
            for e in range(energies):
                total[kind, e] += term(2, e, halo[1, kind, e])

        parts = [total[kind, e].reshape(owners, per_energy, width) for e in range(energies)]
        g_send[kind] = jnp.concatenate(parts, 1).astype(BF16)
        spread(g_send.at[kind], g_recv.at[kind], g_out.at[kind], g_in.at[kind])
        g_recv[kind, me] = g_send[kind, me]

    def transform(pieces):
        return dot(tab_v[:, : flat * len(pieces)], jnp.concatenate(pieces, 0))

    def forward(values):
        turned = widen(values)
        return transform([values, turned, values, turned])

    factor = 1.0 / (count * math.sqrt(count))

    def convolve(kind):
        wait_all(g_recv.at[kind], g_in.at[kind])
        green_hat = forward(g_recv[kind].reshape(flat, width))
        product = complex_times(green_hat, screen_hat[kind])
        turned = times_i(product)
        high, turned_high = product.astype(BF16), turned.astype(BF16)
        low = (product - high.astype(F32)).astype(BF16)
        turned_low = (turned - turned_high.astype(F32)).astype(BF16)
        sigma = transform([turned_high, high, turned_high, high, turned_low, low])
        c_send[kind] = (sigma * factor).astype(BF16).reshape(owners, chunk, width)
        spread(c_send.at[kind], back.at[kind], c_out.at[kind], c_in.at[kind])
        own = pltpu.make_async_copy(c_send.at[kind, me], back.at[kind, me], own_sem.at[kind])
        own.start()
        return own

    green(0)
    loads[6].wait()
    wait_all(s_recv, s_in)
    for kind in range(2):
        screen_hat[kind] = forward(s_recv[:, kind].reshape(flat, width))
    green(1)
    owns = [convolve(0), convolve(1)]

    loads[7].wait()
    for e in range(energies):
        places_v[e] = one_hot(key_col, row_v[e])
    store = pltpu.make_async_copy(places_v, places, store_sem)
    store.start()

    for kind in range(2):
        @pl.when(has_right)
        def _():
            halo_copy(0, kind).wait_send()

        @pl.when(has_left)
        def _():
            halo_copy(1, kind).wait_send()

    wait_all(s_send, s_out)
    for kind in range(2):
        wait_all(g_send.at[kind], g_out.at[kind])
        wait_all(c_send.at[kind], c_out.at[kind])
        wait_all(back.at[kind], c_in.at[kind])
        owns[kind].wait()
    store.wait()


def expand(back, places, result):
    energies, kinds = result.shape[:2]
    for kind in range(kinds):
        rows = back[kind].reshape(-1, back.shape[-1])
        for e in range(energies):
            result[e, kind] = dot(places[e], rows).astype(BF16)


def layout(owners, energies, live):
    share = -(-live // owners)
    padded = -(-share // 8) * 8
    while energies * padded % 16:
        padded += 8
    slot = np.arange(owners * padded)
    wanted = slot // padded * share + slot % padded
    wanted = np.where((slot % padded < share) & (wanted < live), wanted, -2)
    by_energy = np.full((energies, owners, energies, padded), -2)
    for e in range(energies):
        by_energy[e, :, e] = wanted.reshape(owners, padded)
    by_energy = by_energy.reshape(energies, -1)
    count = owners * energies
    index = np.arange(count)
    angle = 2.0 * np.pi / count * (index[:, None] * index[None, :] % count)
    tables = np.stack([np.cos(angle), np.sin(angle)]).astype(np.float32)
    high = tables.astype(jnp.bfloat16)
    low = (tables - high.astype(np.float32)).astype(jnp.bfloat16)
    small = np.concatenate([high, low]).astype(np.float32)
    eye = np.eye(padded, dtype=np.float32)
    cos_high, sin_high, cos_low, sin_low = [np.kron(table, eye) for table in small]
    wide = [cos_high, -sin_high, cos_low, -sin_low, cos_high, -sin_high]
    wide = np.concatenate(wide, 1).astype(jnp.bfloat16)
    return padded, wanted.astype(np.float32), by_energy.astype(np.float32), wide


def local(retarded, injection, screened, pattern):
    energies, _, block, width = retarded.shape
    owners = lax.axis_size("energy")
    live = block * 2 // 3
    padded, wanted, by_energy, tables = layout(owners, energies, live)
    chunk = energies * padded
    flat = owners * chunk
    slots = owners * padded
    anywhere = pl.BlockSpec(memory_space=pl.ANY)
    vmem = pl.BlockSpec(memory_space=pltpu.VMEM)
    dma = pltpu.SemaphoreType.DMA
    blocks = (2, owners, chunk, width)
    back, places = pl.pallas_call(
        kernel,
        out_shape=(
            jax.ShapeDtypeStruct(blocks, BF16),
            jax.ShapeDtypeStruct((energies, block, flat), BF16),
        ),
        in_specs=[anywhere] * 8,
        out_specs=(anywhere, anywhere),
        scratch_shapes=[
            pltpu.VMEM(retarded.shape, BF16),
            pltpu.VMEM(injection.shape, BF16),
            pltpu.VMEM(screened.shape, BF16),
            pltpu.VMEM((1, block), pattern.dtype),
            pltpu.VMEM(tables.shape, BF16),
            pltpu.VMEM((slots, 1), F32),
            pltpu.VMEM((energies, flat, 1), F32),
            pltpu.VMEM((energies, 1, flat), F32),
            pltpu.VMEM((2, 2, energies, block, width), BF16),
            pltpu.VMEM((3, energies, 2 * block, width), BF16),
            pltpu.VMEM((3, energies, slots, width), BF16),
            pltpu.VMEM((2, energies, slots, width), F32),
            pltpu.VMEM((2, flat, width), F32),
            pltpu.VMEM((energies, block, flat), BF16),
            pltpu.VMEM((owners, 2, chunk, width), BF16),
            pltpu.VMEM((owners, 2, chunk, width), BF16),
            pltpu.VMEM(blocks, BF16),
            pltpu.VMEM(blocks, BF16),
            pltpu.VMEM(blocks, BF16),
            dma((8,)),
            dma((2, 2)),
            dma((2, 2)),
            dma,
            dma,
            dma((2,)),
            dma((2,)),
            dma((2,)),
            dma((2,)),
            dma((2,)),
            dma,
        ],
        compiler_params=pltpu.CompilerParams(
            collective_id=0, has_side_effects=True, vmem_limit_bytes=56 * 1024 * 1024
        ),
    )(
        retarded,
        injection,
        screened,
        pattern.reshape(1, -1),
        jnp.asarray(tables),
        jnp.asarray(wanted.reshape(-1, 1)),
        jnp.asarray(by_energy.reshape(energies, -1, 1)),
        jnp.asarray(by_energy.reshape(energies, 1, -1)),
    )
    return pl.pallas_call(
        expand,
        out_shape=jax.ShapeDtypeStruct(screened.shape, BF16),
        in_specs=[vmem, vmem],
        out_specs=vmem,
        compiler_params=pltpu.CompilerParams(vmem_limit_bytes=32 * 1024 * 1024),
    )(back, places)


def solution(mesh):
    placed = (
        P("energy", None, "slab", None),
        P("energy", None, "slab", None),
        P("energy", None, "slab", None),
        P("slab"),
    )
    return jax.shard_map(
        local,
        mesh=mesh,
        in_specs=placed,
        out_specs=P("energy", None, "slab", None),
        check_vma=False,
    )
```

```python
import functools
import math

import jax
import jax.numpy as jnp
import numpy as np
from jax import lax
from jax.experimental import pallas as pl
from jax.experimental.pallas import tpu as pltpu
from jax.sharding import PartitionSpec as P

MESH = pl.DeviceIdType.MESH
F32 = jnp.float32
BF16 = jnp.bfloat16


def dot(a, b):
    return jnp.dot(a, b, preferred_element_type=F32)


def dot_nt(a, b):
    return lax.dot_general(a, b, (((1,), (1,)), ((), ())), preferred_element_type=F32)


def times_i(x):
    half = x.shape[-1] // 2
    lane = lax.broadcasted_iota(jnp.int32, x.shape, 1)
    turned = pltpu.roll(x, half, 1)
    return jnp.where(lane < half, -turned, turned)


def complex_times(x, y):
    half = x.shape[-1] // 2
    first = lax.broadcasted_iota(jnp.int32, x.shape, 1) < half
    turned = pltpu.roll(y, half, 1)
    return x * jnp.where(first, y, turned) + times_i(x) * jnp.where(first, turned, y)


def kernel(
    live, padded,
    retarded, injection, screened, pattern, tables,
    back, places,
    ret_v, inj_v, scr_v, pat_v, tab_v,
    halo, row_wide, row_live, total, screen_hat,
    s_send, s_recv, g_send, g_recv, c_send,
    load_sem, halo_out, halo_in, s_out, s_in, g_out, g_in, c_out, c_in, own_sem,
):
    owners = lax.axis_size("energy")
    slabs = lax.axis_size("slab")
    me = lax.axis_index("energy")
    slab = lax.axis_index("slab")
    has_left = slab > 0
    has_right = slab < slabs - 1
    energies, _, block, width = ret_v.shape
    chunk = s_send.shape[2]
    per_energy = chunk // energies
    flat = owners * chunk
    count = owners * energies

    share = -(-live // owners)
    far, near = [owners // 2], []
    while far[0] >> len(near) > 1:
        near.append(far[0] >> len(near) + 1)

    loads = [
        pltpu.make_async_copy(source, target, load_sem.at[at])
        for at, (source, target) in enumerate(
            [
                (pattern, pat_v),
                (screened, scr_v),
                (retarded, ret_v),
                (injection, inj_v),
                (tables, tab_v),
            ]
        )
    ]
    for load in loads:
        load.start()

    barrier = pltpu.get_barrier_semaphore()

    def greet(step, carry):
        peer = lax.rem(me + step, owners)
        pl.semaphore_signal(barrier, inc=1, device_id={"energy": peer}, device_id_type=MESH)
        return carry

    lax.fori_loop(1, owners, greet, 0)

    @pl.when(has_left)
    def _():
        pl.semaphore_signal(barrier, inc=1, device_id={"slab": slab - 1}, device_id_type=MESH)

    @pl.when(has_right)
    def _():
        pl.semaphore_signal(barrier, inc=1, device_id={"slab": slab + 1}, device_id_type=MESH)

    def spread(source, target, out_sem, in_sem, halves=None):
        for half in halves or far + near:
            group = me // half
            first = (group + 1 - 2 * lax.rem(group, 2)) * half

            def send(step, carry, half=half, first=first):
                peer = first + lax.rem(me + step, half)
                pltpu.make_async_remote_copy(
                    src_ref=source.at[peer],
                    dst_ref=target.at[me],
                    send_sem=out_sem,
                    recv_sem=in_sem,
                    device_id={"energy": peer},
                    device_id_type=MESH,
                ).start()
                return carry

            lax.fori_loop(0, half, send, 0)

    def wait_all(buffer, sem):
        rest = buffer.at[pl.ds(0, owners - 1)]
        pltpu.make_async_copy(rest, rest, sem).wait()

    loads[0].wait()
    pattern_row = pat_v[...].astype(F32)
    down = lax.broadcasted_iota(jnp.int32, (block, block), 0)
    across = lax.broadcasted_iota(jnp.int32, (block, block), 1)
    pattern_col = jnp.sum(jnp.where(down == across, pattern_row, 0.0), 1, keepdims=True)
    rank_col = jnp.sum(jnp.where(across < down, pattern_row, 0.0), 1, keepdims=True)
    rank_row = jnp.sum(jnp.where(down < across, pattern_col, 0.0), 0, keepdims=True)
    key_col = jnp.where(pattern_col > 0.5, rank_col, -1.0)
    key_row = jnp.where(pattern_row > 0.5, rank_row, -1.0)

    def one_hot(left, right):
        return jnp.where(left == right, 1.0, 0.0).astype(BF16)

    def wanted(shape, axis, size, energy):
        at = lax.broadcasted_iota(jnp.int32, shape, axis).astype(F32)
        owner = jnp.floor((at + 0.5) * (1.0 / size))
        inside = at - owner * size - energy * padded
        row = owner * share + inside
        return jnp.where((inside >= 0) & (inside < share) & (row < live), row, -2.0)

    picks = [one_hot(wanted((flat, 1), 0, chunk, e), key_row) for e in range(energies)]
    loads[1].wait()
    for kind in range(2):
        picked = sum(dot(picks[e], scr_v[e, kind]) for e in range(energies))
        s_send[:, kind] = picked.astype(BF16).reshape(owners, chunk, width)

    pl.semaphore_wait(
        barrier, owners - 1 + has_left.astype(jnp.int32) + has_right.astype(jnp.int32)
    )

    def halo_copy(side, kind):
        return pltpu.make_async_remote_copy(
            src_ref=injection.at[:, kind],
            dst_ref=halo.at[side, kind],
            send_sem=halo_out.at[side, kind],
            recv_sem=halo_in.at[side, kind],
            device_id={"slab": slab + 1 - 2 * side},
            device_id_type=MESH,
        )

    for kind in range(2):
        @pl.when(has_right)
        def _():
            halo_copy(0, kind).start()

        @pl.when(has_left)
        def _():
            halo_copy(1, kind).start()

    spread(s_send, s_recv, s_out, s_in)
    s_recv[me] = s_send[me]

    pick_rows = one_hot(wanted((owners * padded, 1), 0, padded, 0), key_row)

    def widen(x):
        return times_i(x.astype(F32)).astype(BF16)

    def prepare(offset):
        for e in range(energies):
            rows = ret_v[e, offset]
            row_wide[offset, e, :block] = rows
            row_wide[offset, e, block:] = widen(rows)
            row_live[offset, e] = dot(pick_rows, rows).astype(BF16)

    def term(offset, e, inject):
        expanded = jnp.concatenate([inject, widen(inject)], 0)
        left = dot(row_live[offset, e], expanded).astype(BF16)
        return dot_nt(left, row_wide[offset, e])

    loads[2].wait()
    loads[3].wait()
    prepare(1)

    @pl.when(has_left)
    def _():
        prepare(0)

    @pl.when(has_right)
    def _():
        prepare(2)

    for kind in range(2):
        for e in range(energies):
            total[kind, e] = term(1, e, inj_v[e, kind])

    def green(kind):
        @pl.when(has_left)
        def _():
            halo_copy(0, kind).wait_recv()
            for e in range(energies):
                total[kind, e] += term(0, e, halo[0, kind, e])

        @pl.when(has_right)
        def _():
            halo_copy(1, kind).wait_recv()
            for e in range(energies):
                total[kind, e] += term(2, e, halo[1, kind, e])

        parts = [total[kind, e].reshape(owners, per_energy, width) for e in range(energies)]
        g_send[kind] = jnp.concatenate(parts, 1).astype(BF16)
        spread(g_send.at[kind], g_recv.at[kind], g_out.at[kind], g_in.at[kind])
        g_recv[kind, me] = g_send[kind, me]

    def transform(pieces):
        return dot(tab_v[:, : flat * len(pieces)], jnp.concatenate(pieces, 0))

    def forward(values):
        turned = widen(values)
        return transform([values, turned, values, turned])

    factor = 1.0 / (count * math.sqrt(count))

    def convolve(kind):
        green_hat = forward(g_recv[kind].reshape(flat, width))
        product = complex_times(green_hat, screen_hat[kind])
        turned = times_i(product)
        high, turned_high = product.astype(BF16), turned.astype(BF16)
        low = (product - high.astype(F32)).astype(BF16)
        turned_low = (turned - turned_high.astype(F32)).astype(BF16)
        sigma = transform([turned_high, high, turned_high, high, turned_low, low])
        c_send[kind] = (sigma * factor).astype(BF16).reshape(owners, chunk, width)

    def give_back(kind, halves):
        spread(c_send.at[kind], back.at[kind], c_out.at[kind], c_in.at[kind], halves)

    def keep_own(kind):
        own = pltpu.make_async_copy(c_send.at[kind, me], back.at[kind, me], own_sem.at[kind])
        own.start()
        return own

    green(0)
    loads[4].wait()
    wait_all(s_recv, s_in)
    for kind in range(2):
        screen_hat[kind] = forward(s_recv[:, kind].reshape(flat, width))
    green(1)
    wait_all(g_recv.at[0], g_in.at[0])
    convolve(0)
    give_back(0, near)
    wait_all(g_recv.at[1], g_in.at[1])
    give_back(0, far)
    convolve(1)
    give_back(1, far + near)
    owns = [keep_own(0), keep_own(1)]
    for e in range(energies):
        places[e] = one_hot(key_col, wanted((1, flat), 1, chunk, e))

    for kind in range(2):
        @pl.when(has_right)
        def _():
            halo_copy(0, kind).wait_send()

        @pl.when(has_left)
        def _():
            halo_copy(1, kind).wait_send()

    wait_all(s_send, s_out)
    for kind in range(2):
        wait_all(g_send.at[kind], g_out.at[kind])
        wait_all(c_send.at[kind], c_out.at[kind])
        wait_all(back.at[kind], c_in.at[kind])
        owns[kind].wait()


def expand(back, places, result):
    energies, kinds = result.shape[:2]
    for kind in range(kinds):
        rows = back[kind].reshape(-1, back.shape[-1])
        for e in range(energies):
            result[e, kind] = dot(places[e], rows).astype(BF16)


def transform_tables(count, padded):
    index = np.arange(count)
    angle = 2.0 * np.pi / count * (index[:, None] * index[None, :] % count)
    tables = np.stack([np.cos(angle), -np.sin(angle)]).astype(np.float32)
    high = tables.astype(jnp.bfloat16).astype(np.float32)
    low = (tables - high).astype(jnp.bfloat16).astype(np.float32)
    eye = np.eye(padded, dtype=np.float32)
    wide = [np.kron(table, eye) for table in (*high, *low, *high)]
    return np.concatenate(wide, 1).astype(jnp.bfloat16)


def local(retarded, injection, screened, pattern):
    energies, _, block, width = retarded.shape
    owners = lax.axis_size("energy")
    live = block * 2 // 3
    padded = -(-live // (owners * 8)) * 8
    while energies * padded % 16:
        padded += 8
    tables = transform_tables(owners * energies, padded)
    chunk = energies * padded
    flat = owners * chunk
    slots = owners * padded
    anywhere = pl.BlockSpec(memory_space=pl.ANY)
    vmem = pl.BlockSpec(memory_space=pltpu.VMEM)
    dma = pltpu.SemaphoreType.DMA
    blocks = (2, owners, chunk, width)
    back, places = pl.pallas_call(
        functools.partial(kernel, live, padded),
        out_shape=(
            jax.ShapeDtypeStruct(blocks, BF16),
            jax.ShapeDtypeStruct((energies, block, flat), BF16),
        ),
        in_specs=[anywhere] * 5,
        out_specs=(vmem, vmem),
        scratch_shapes=[
            pltpu.VMEM(retarded.shape, BF16),
            pltpu.VMEM(injection.shape, BF16),
            pltpu.VMEM(screened.shape, BF16),
            pltpu.VMEM((1, block), pattern.dtype),
            pltpu.VMEM(tables.shape, BF16),
            pltpu.VMEM((2, 2, energies, block, width), BF16),
            pltpu.VMEM((3, energies, 2 * block, width), BF16),
            pltpu.VMEM((3, energies, slots, width), BF16),
            pltpu.VMEM((2, energies, slots, width), F32),
            pltpu.VMEM((2, flat, width), F32),
            pltpu.VMEM((owners, 2, chunk, width), BF16),
            pltpu.VMEM((owners, 2, chunk, width), BF16),
            pltpu.VMEM(blocks, BF16),
            pltpu.VMEM(blocks, BF16),
            pltpu.VMEM(blocks, BF16),
            dma((5,)),
            dma((2, 2)),
            dma((2, 2)),
            dma,
            dma,
            dma((2,)),
            dma((2,)),
            dma((2,)),
            dma((2,)),
            dma((2,)),
        ],
        compiler_params=pltpu.CompilerParams(
            collective_id=0, has_side_effects=True, vmem_limit_bytes=53 * 1024 * 1024
        ),
    )(
        retarded,
        injection,
        screened,
        pattern.reshape(1, -1),
        jnp.asarray(tables),
    )
    return pl.pallas_call(
        expand,
        out_shape=jax.ShapeDtypeStruct(screened.shape, BF16),
        in_specs=[vmem, vmem],
        out_specs=vmem,
        compiler_params=pltpu.CompilerParams(vmem_limit_bytes=32 * 1024 * 1024),
    )(back, places)


def solution(mesh):
    placed = (
        P("energy", None, "slab", None),
        P("energy", None, "slab", None),
        P("energy", None, "slab", None),
        P("slab"),
    )
    return jax.shard_map(
        local,
        mesh=mesh,
        in_specs=placed,
        out_specs=P("energy", None, "slab", None),
        check_vma=False,
    )
```

```python
import functools
import math

import jax
import jax.numpy as jnp
import numpy as np
from jax import lax
from jax.experimental import pallas as pl
from jax.experimental.pallas import tpu as pltpu
from jax.sharding import PartitionSpec as P

MESH = pl.DeviceIdType.MESH
F32 = jnp.float32
BF16 = jnp.bfloat16


def dot(a, b):
    return jnp.dot(a, b, preferred_element_type=F32)


def dot_nt(a, b):
    return lax.dot_general(a, b, (((1,), (1,)), ((), ())), preferred_element_type=F32)


def times_i(x):
    half = x.shape[-1] // 2
    lane = lax.broadcasted_iota(jnp.int32, x.shape, 1)
    turned = pltpu.roll(x, half, 1)
    return jnp.where(lane < half, -turned, turned)


def complex_times(x, y):
    half = x.shape[-1] // 2
    first = lax.broadcasted_iota(jnp.int32, x.shape, 1) < half
    turned = pltpu.roll(y, half, 1)
    return x * jnp.where(first, y, turned) + times_i(x) * jnp.where(first, turned, y)


def kernel(
    live, padded,
    retarded, injection, screened, pattern, tables,
    back, places,
    ret_v, inj_v, scr_v, pat_v, tab_v,
    halo, row_wide, row_live, total, screen_hat,
    s_send, s_recv, g_send, g_recv, c_send,
    load_sem, halo_out, halo_in, s_out, s_in, g_out, g_in, c_out, c_in, own_sem,
):
    owners = lax.axis_size("energy")
    slabs = lax.axis_size("slab")
    me = lax.axis_index("energy")
    slab = lax.axis_index("slab")
    has_left = slab > 0
    has_right = slab < slabs - 1
    energies, _, block, width = ret_v.shape
    chunk = s_send.shape[2]
    per_energy = chunk // energies
    flat = owners * chunk
    count = owners * energies

    share = -(-live // owners)
    loads = [
        pltpu.make_async_copy(source, target, load_sem.at[at])
        for at, (source, target) in enumerate(
            [
                (pattern, pat_v),
                (screened, scr_v),
                (retarded, ret_v),
                (injection, inj_v),
                (tables, tab_v),
            ]
        )
    ]
    for load in loads:
        load.start()

    barrier = pltpu.get_barrier_semaphore()

    def greet(step, carry):
        peer = lax.rem(me + step, owners)
        pl.semaphore_signal(barrier, inc=1, device_id={"energy": peer}, device_id_type=MESH)
        return carry

    lax.fori_loop(1, owners, greet, 0)

    @pl.when(has_left)
    def _():
        pl.semaphore_signal(barrier, inc=1, device_id={"slab": slab - 1}, device_id_type=MESH)

    @pl.when(has_right)
    def _():
        pl.semaphore_signal(barrier, inc=1, device_id={"slab": slab + 1}, device_id_type=MESH)

    def spread(source, target, out_sem, in_sem):
        half = owners // 2
        mine = me // half * half

        def send(peer):
            pltpu.make_async_remote_copy(
                src_ref=source.at[peer],
                dst_ref=target.at[me],
                send_sem=out_sem,
                recv_sem=in_sem,
                device_id={"energy": peer},
                device_id_type=MESH,
            ).start()

        def pair(step, carry):
            turn = lax.rem(me + step, half)
            send(half - mine + turn)
            send(mine + turn)
            return carry

        send(half - mine + lax.rem(me, half))
        lax.fori_loop(1, half, pair, 0)

    def wait_all(buffer, sem):
        rest = buffer.at[pl.ds(0, owners - 1)]
        pltpu.make_async_copy(rest, rest, sem).wait()

    pl.semaphore_wait(
        barrier, owners - 1 + has_left.astype(jnp.int32) + has_right.astype(jnp.int32)
    )

    def halo_copy(side, kind):
        return pltpu.make_async_remote_copy(
            src_ref=injection.at[:, kind],
            dst_ref=halo.at[side, kind],
            send_sem=halo_out.at[side, kind],
            recv_sem=halo_in.at[side, kind],
            device_id={"slab": slab + 1 - 2 * side},
            device_id_type=MESH,
        )

    for kind in range(2):
        @pl.when(has_right)
        def _():
            halo_copy(0, kind).start()

        @pl.when(has_left)
        def _():
            halo_copy(1, kind).start()

    loads[0].wait()
    pattern_row = pat_v[...].astype(F32)
    down = lax.broadcasted_iota(jnp.int32, (block, block), 0)
    across = lax.broadcasted_iota(jnp.int32, (block, block), 1)
    pattern_col = jnp.sum(jnp.where(down == across, pattern_row, 0.0), 1, keepdims=True)
    rank_col = jnp.sum(jnp.where(across < down, pattern_row, 0.0), 1, keepdims=True)
    rank_row = jnp.sum(jnp.where(down < across, pattern_col, 0.0), 0, keepdims=True)
    key_col = jnp.where(pattern_col > 0.5, rank_col, -1.0)
    key_row = jnp.where(pattern_row > 0.5, rank_row, -1.0)

    def one_hot(left, right):
        return jnp.where(left == right, 1.0, 0.0).astype(BF16)

    def wanted(shape, axis, size, energy):
        at = lax.broadcasted_iota(jnp.int32, shape, axis).astype(F32)
        owner = jnp.floor((at + 0.5) * (1.0 / size))
        inside = at - owner * size - energy * padded
        row = owner * share + inside
        return jnp.where((inside >= 0) & (inside < share) & (row < live), row, -2.0)

    picks = [one_hot(wanted((flat, 1), 0, chunk, e), key_row) for e in range(energies)]
    loads[1].wait()
    for kind in range(2):
        picked = sum(dot(picks[e], scr_v[e, kind]) for e in range(energies))
        s_send[:, kind] = picked.astype(BF16).reshape(owners, chunk, width)

    spread(s_send, s_recv, s_out, s_in)
    s_recv[me] = s_send[me]

    pick_rows = one_hot(wanted((owners * padded, 1), 0, padded, 0), key_row)

    def widen(x):
        return times_i(x.astype(F32)).astype(BF16)

    def prepare(offset):
        for e in range(energies):
            rows = ret_v[e, offset]
            row_wide[offset, e, :block] = rows
            row_wide[offset, e, block:] = widen(rows)
            row_live[offset, e] = dot(pick_rows, rows).astype(BF16)

    def term(offset, e, inject):
        expanded = jnp.concatenate([inject, widen(inject)], 0)
        left = dot(row_live[offset, e], expanded).astype(BF16)
        return dot_nt(left, row_wide[offset, e])

    loads[2].wait()
    loads[3].wait()
    prepare(1)

    @pl.when(has_left)
    def _():
        prepare(0)

    @pl.when(has_right)
    def _():
        prepare(2)

    for kind in range(2):
        for e in range(energies):
            total[kind, e] = term(1, e, inj_v[e, kind])

    def green(kind):
        @pl.when(has_left)
        def _():
            halo_copy(0, kind).wait_recv()
            for e in range(energies):
                total[kind, e] += term(0, e, halo[0, kind, e])

        @pl.when(has_right)
        def _():
            halo_copy(1, kind).wait_recv()
            for e in range(energies):
                total[kind, e] += term(2, e, halo[1, kind, e])

        parts = [total[kind, e].reshape(owners, per_energy, width) for e in range(energies)]
        g_send[kind] = jnp.concatenate(parts, 1).astype(BF16)
        spread(g_send.at[kind], g_recv.at[kind], g_out.at[kind], g_in.at[kind])
        g_recv[kind, me] = g_send[kind, me]

    def transform(pieces):
        return dot(tab_v[:, : flat * len(pieces)], jnp.concatenate(pieces, 0))

    def forward(values):
        turned = widen(values)
        return transform([values, turned, values, turned])

    factor = 1.0 / (count * math.sqrt(count))

    def convolve(kind):
        wait_all(g_recv.at[kind], g_in.at[kind])
        green_hat = forward(g_recv[kind].reshape(flat, width))
        product = complex_times(green_hat, screen_hat[kind])
        turned = times_i(product)
        high, turned_high = product.astype(BF16), turned.astype(BF16)
        low = (product - high.astype(F32)).astype(BF16)
        turned_low = (turned - turned_high.astype(F32)).astype(BF16)
        sigma = transform([turned_high, high, turned_high, high, turned_low, low])
        c_send[kind] = (sigma * factor).astype(BF16).reshape(owners, chunk, width)
        spread(c_send.at[kind], back.at[kind], c_out.at[kind], c_in.at[kind])

    def keep_own(kind):
        own = pltpu.make_async_copy(c_send.at[kind, me], back.at[kind, me], own_sem.at[kind])
        own.start()
        return own

    green(0)
    loads[4].wait()
    wait_all(s_recv, s_in)
    for kind in range(2):
        screen_hat[kind] = forward(s_recv[:, kind].reshape(flat, width))
    green(1)
    convolve(0)
    convolve(1)
    owns = [keep_own(0), keep_own(1)]
    for e in range(energies):
        places[e] = one_hot(key_col, wanted((1, flat), 1, chunk, e))

    for kind in range(2):
        @pl.when(has_right)
        def _():
            halo_copy(0, kind).wait_send()

        @pl.when(has_left)
        def _():
            halo_copy(1, kind).wait_send()

    wait_all(s_send, s_out)
    for kind in range(2):
        wait_all(g_send.at[kind], g_out.at[kind])
        wait_all(c_send.at[kind], c_out.at[kind])
        wait_all(back.at[kind], c_in.at[kind])
        owns[kind].wait()


def expand(back, places, result):
    energies, kinds = result.shape[:2]
    for kind in range(kinds):
        rows = back[kind].reshape(-1, back.shape[-1])
        for e in range(energies):
            result[e, kind] = dot(places[e], rows).astype(BF16)


def transform_tables(count, padded):
    index = np.arange(count)
    angle = 2.0 * np.pi / count * (index[:, None] * index[None, :] % count)
    tables = np.stack([np.cos(angle), -np.sin(angle)]).astype(np.float32)
    high = tables.astype(jnp.bfloat16).astype(np.float32)
    low = (tables - high).astype(jnp.bfloat16).astype(np.float32)
    eye = np.eye(padded, dtype=np.float32)
    wide = [np.kron(table, eye) for table in (*high, *low, *high)]
    return np.concatenate(wide, 1).astype(jnp.bfloat16)


def local(retarded, injection, screened, pattern):
    energies, _, block, width = retarded.shape
    owners = lax.axis_size("energy")
    live = block * 2 // 3
    padded = -(-live // (owners * 8)) * 8
    while energies * padded % 16:
        padded += 8
    tables = transform_tables(owners * energies, padded)
    chunk = energies * padded
    flat = owners * chunk
    slots = owners * padded
    anywhere = pl.BlockSpec(memory_space=pl.ANY)
    vmem = pl.BlockSpec(memory_space=pltpu.VMEM)
    dma = pltpu.SemaphoreType.DMA
    blocks = (2, owners, chunk, width)
    back, places = pl.pallas_call(
        functools.partial(kernel, live, padded),
        out_shape=(
            jax.ShapeDtypeStruct(blocks, BF16),
            jax.ShapeDtypeStruct((energies, block, flat), BF16),
        ),
        in_specs=[anywhere] * 5,
        out_specs=(vmem, vmem),
        scratch_shapes=[
            pltpu.VMEM(retarded.shape, BF16),
            pltpu.VMEM(injection.shape, BF16),
            pltpu.VMEM(screened.shape, BF16),
            pltpu.VMEM((1, block), pattern.dtype),
            pltpu.VMEM(tables.shape, BF16),
            pltpu.VMEM((2, 2, energies, block, width), BF16),
            pltpu.VMEM((3, energies, 2 * block, width), BF16),
            pltpu.VMEM((3, energies, slots, width), BF16),
            pltpu.VMEM((2, energies, slots, width), F32),
            pltpu.VMEM((2, flat, width), F32),
            pltpu.VMEM((owners, 2, chunk, width), BF16),
            pltpu.VMEM((owners, 2, chunk, width), BF16),
            pltpu.VMEM(blocks, BF16),
            pltpu.VMEM(blocks, BF16),
            pltpu.VMEM(blocks, BF16),
            dma((5,)),
            dma((2, 2)),
            dma((2, 2)),
            dma,
            dma,
            dma((2,)),
            dma((2,)),
            dma((2,)),
            dma((2,)),
            dma((2,)),
        ],
        compiler_params=pltpu.CompilerParams(
            collective_id=0, has_side_effects=True, vmem_limit_bytes=53 * 1024 * 1024
        ),
    )(
        retarded,
        injection,
        screened,
        pattern.reshape(1, -1),
        jnp.asarray(tables),
    )
    return pl.pallas_call(
        expand,
        out_shape=jax.ShapeDtypeStruct(screened.shape, BF16),
        in_specs=[vmem, vmem],
        out_specs=vmem,
        compiler_params=pltpu.CompilerParams(vmem_limit_bytes=32 * 1024 * 1024),
    )(back, places)


def solution(mesh):
    placed = (
        P("energy", None, "slab", None),
        P("energy", None, "slab", None),
        P("energy", None, "slab", None),
        P("slab"),
    )
    return jax.shard_map(
        local,
        mesh=mesh,
        in_specs=placed,
        out_specs=P("energy", None, "slab", None),
        check_vma=False,
    )
```

```python
import functools
import math

import jax
import jax.numpy as jnp
import numpy as np
from jax import lax
from jax.experimental import pallas as pl
from jax.experimental.pallas import tpu as pltpu
from jax.sharding import PartitionSpec as P

MESH = pl.DeviceIdType.MESH
F32 = jnp.float32
BF16 = jnp.bfloat16


def dot(a, b):
    return jnp.dot(a, b, preferred_element_type=F32)


def dot_nt(a, b):
    return lax.dot_general(a, b, (((1,), (1,)), ((), ())), preferred_element_type=F32)


def times_i(x):
    half = x.shape[-1] // 2
    lane = lax.broadcasted_iota(jnp.int32, x.shape, 1)
    turned = pltpu.roll(x, half, 1)
    return jnp.where(lane < half, -turned, turned)


def complex_times(x, y):
    half = x.shape[-1] // 2
    first = lax.broadcasted_iota(jnp.int32, x.shape, 1) < half
    turned = pltpu.roll(y, half, 1)
    return x * jnp.where(first, y, turned) + times_i(x) * jnp.where(first, turned, y)


def kernel(
    live, padded,
    retarded, injection, screened, pattern, tables,
    back, places,
    ret_v, inj_v, scr_v, pat_v, tab_v,
    halo, row_wide, row_live, total, screen_hat,
    s_send, s_recv, g_send, g_recv, c_send,
    load_sem, halo_out, halo_in, s_out, s_in, g_out, g_in, c_out, c_in, own_sem,
):
    owners = lax.axis_size("energy")
    slabs = lax.axis_size("slab")
    me = lax.axis_index("energy")
    slab = lax.axis_index("slab")
    has_left = slab > 0
    has_right = slab < slabs - 1
    energies, _, block, width = ret_v.shape
    chunk = s_send.shape[2]
    per_energy = chunk // energies
    flat = owners * chunk
    count = owners * energies

    share = -(-live // owners)
    loads = [
        pltpu.make_async_copy(source, target, load_sem.at[at])
        for at, (source, target) in enumerate(
            [
                (pattern, pat_v),
                (screened, scr_v),
                (retarded, ret_v),
                (injection, inj_v),
                (tables, tab_v),
            ]
        )
    ]
    for load in loads:
        load.start()

    barrier = pltpu.get_barrier_semaphore()

    def greet(step, carry):
        peer = lax.rem(me + step, owners)
        pl.semaphore_signal(barrier, inc=1, device_id={"energy": peer}, device_id_type=MESH)
        return carry

    lax.fori_loop(1, owners, greet, 0)

    @pl.when(has_left)
    def _():
        pl.semaphore_signal(barrier, inc=1, device_id={"slab": slab - 1}, device_id_type=MESH)

    @pl.when(has_right)
    def _():
        pl.semaphore_signal(barrier, inc=1, device_id={"slab": slab + 1}, device_id_type=MESH)

    def spread(source, target, out_sem, in_sem):
        def send(step, carry):
            peer = lax.rem(me + step, owners)
            pltpu.make_async_remote_copy(
                src_ref=source.at[peer],
                dst_ref=target.at[me],
                send_sem=out_sem,
                recv_sem=in_sem,
                device_id={"energy": peer},
                device_id_type=MESH,
            ).start()
            return carry

        lax.fori_loop(1, owners, send, 0)

    def wait_all(buffer, sem):
        rest = buffer.at[pl.ds(0, owners - 1)]
        pltpu.make_async_copy(rest, rest, sem).wait()

    pl.semaphore_wait(
        barrier, owners - 1 + has_left.astype(jnp.int32) + has_right.astype(jnp.int32)
    )

    def halo_copy(side, kind):
        return pltpu.make_async_remote_copy(
            src_ref=injection.at[:, kind],
            dst_ref=halo.at[side, kind],
            send_sem=halo_out.at[side, kind],
            recv_sem=halo_in.at[side, kind],
            device_id={"slab": slab + 1 - 2 * side},
            device_id_type=MESH,
        )

    def send_halo(kind):
        @pl.when(has_right)
        def _():
            halo_copy(0, kind).start()

        @pl.when(has_left)
        def _():
            halo_copy(1, kind).start()

    def take_halo(kind):
        @pl.when(has_left)
        def _():
            halo_copy(0, kind).wait_recv()

        @pl.when(has_right)
        def _():
            halo_copy(1, kind).wait_recv()

    send_halo(0)

    loads[0].wait()
    pattern_row = pat_v[...].astype(F32)
    down = lax.broadcasted_iota(jnp.int32, (block, block), 0)
    across = lax.broadcasted_iota(jnp.int32, (block, block), 1)
    pattern_col = jnp.sum(jnp.where(down == across, pattern_row, 0.0), 1, keepdims=True)
    rank_col = jnp.sum(jnp.where(across < down, pattern_row, 0.0), 1, keepdims=True)
    rank_row = jnp.sum(jnp.where(down < across, pattern_col, 0.0), 0, keepdims=True)
    key_col = jnp.where(pattern_col > 0.5, rank_col, -1.0)
    key_row = jnp.where(pattern_row > 0.5, rank_row, -1.0)

    def one_hot(left, right):
        return jnp.where(left == right, 1.0, 0.0).astype(BF16)

    def wanted(shape, axis, size, energy):
        at = lax.broadcasted_iota(jnp.int32, shape, axis).astype(F32)
        owner = jnp.floor((at + 0.5) * (1.0 / size))
        inside = at - owner * size - energy * padded
        row = owner * share + inside
        return jnp.where((inside >= 0) & (inside < share) & (row < live), row, -2.0)

    picks = [one_hot(wanted((flat, 1), 0, chunk, e), key_row) for e in range(energies)]
    loads[1].wait()
    for kind in range(2):
        picked = sum(dot(picks[e], scr_v[e, kind]) for e in range(energies))
        s_send[:, kind] = picked.astype(BF16).reshape(owners, chunk, width)

    spread(s_send, s_recv, s_out, s_in)
    s_recv[me] = s_send[me]

    pick_rows = one_hot(wanted((owners * padded, 1), 0, padded, 0), key_row)

    def widen(x):
        return times_i(x.astype(F32)).astype(BF16)

    def prepare(offset):
        for e in range(energies):
            rows = ret_v[e, offset]
            row_wide[offset, e, :block] = rows
            row_wide[offset, e, block:] = widen(rows)
            row_live[offset, e] = dot(pick_rows, rows).astype(BF16)

    def term(offset, e, inject):
        expanded = jnp.concatenate([inject, widen(inject)], 0)
        left = dot(row_live[offset, e], expanded).astype(BF16)
        return dot_nt(left, row_wide[offset, e])

    loads[2].wait()
    loads[3].wait()
    prepare(1)

    @pl.when(has_left)
    def _():
        prepare(0)

    @pl.when(has_right)
    def _():
        prepare(2)

    for kind in range(2):
        for e in range(energies):
            total[kind, e] = term(1, e, inj_v[e, kind])

    def green(kind):
        @pl.when(has_left)
        def _():
            for e in range(energies):
                total[kind, e] += term(0, e, halo[0, kind, e])

        @pl.when(has_right)
        def _():
            for e in range(energies):
                total[kind, e] += term(2, e, halo[1, kind, e])

        parts = [total[kind, e].reshape(owners, per_energy, width) for e in range(energies)]
        g_send[kind] = jnp.concatenate(parts, 1).astype(BF16)
        spread(g_send.at[kind], g_recv.at[kind], g_out.at[kind], g_in.at[kind])
        g_recv[kind, me] = g_send[kind, me]

    def transform(pieces):
        return dot(tab_v[:, : flat * len(pieces)], jnp.concatenate(pieces, 0))

    def forward(values):
        turned = widen(values)
        return transform([values, turned, values, turned])

    factor = 1.0 / (count * math.sqrt(count))

    def convolve(kind):
        wait_all(g_recv.at[kind], g_in.at[kind])
        green_hat = forward(g_recv[kind].reshape(flat, width))
        product = complex_times(green_hat, screen_hat[kind])
        turned = times_i(product)
        high, turned_high = product.astype(BF16), turned.astype(BF16)
        low = (product - high.astype(F32)).astype(BF16)
        turned_low = (turned - turned_high.astype(F32)).astype(BF16)
        sigma = transform([turned_high, high, turned_high, high, turned_low, low])
        c_send[kind] = (sigma * factor).astype(BF16).reshape(owners, chunk, width)
        spread(c_send.at[kind], back.at[kind], c_out.at[kind], c_in.at[kind])

    def keep_own(kind):
        own = pltpu.make_async_copy(c_send.at[kind, me], back.at[kind, me], own_sem.at[kind])
        own.start()
        return own

    take_halo(0)
    send_halo(1)
    green(0)
    loads[4].wait()
    wait_all(s_recv, s_in)
    for kind in range(2):
        screen_hat[kind] = forward(s_recv[:, kind].reshape(flat, width))
    take_halo(1)
    green(1)
    convolve(0)
    convolve(1)
    owns = [keep_own(0), keep_own(1)]
    for e in range(energies):
        places[e] = one_hot(key_col, wanted((1, flat), 1, chunk, e))

    for kind in range(2):
        @pl.when(has_right)
        def _():
            halo_copy(0, kind).wait_send()

        @pl.when(has_left)
        def _():
            halo_copy(1, kind).wait_send()

    wait_all(s_send, s_out)
    for kind in range(2):
        wait_all(g_send.at[kind], g_out.at[kind])
        wait_all(c_send.at[kind], c_out.at[kind])
        wait_all(back.at[kind], c_in.at[kind])
        owns[kind].wait()


def expand(back, places, result):
    energies, kinds = result.shape[:2]
    for kind in range(kinds):
        rows = back[kind].reshape(-1, back.shape[-1])
        for e in range(energies):
            result[e, kind] = dot(places[e], rows).astype(BF16)


def transform_tables(count, padded):
    index = np.arange(count)
    angle = 2.0 * np.pi / count * (index[:, None] * index[None, :] % count)
    tables = np.stack([np.cos(angle), -np.sin(angle)]).astype(np.float32)
    high = tables.astype(jnp.bfloat16).astype(np.float32)
    low = (tables - high).astype(jnp.bfloat16).astype(np.float32)
    eye = np.eye(padded, dtype=np.float32)
    wide = [np.kron(table, eye) for table in (*high, *low, *high)]
    return np.concatenate(wide, 1).astype(jnp.bfloat16)


def local(retarded, injection, screened, pattern):
    energies, _, block, width = retarded.shape
    owners = lax.axis_size("energy")
    live = block * 2 // 3
    padded = -(-live // (owners * 8)) * 8
    while energies * padded % 16:
        padded += 8
    tables = transform_tables(owners * energies, padded)
    chunk = energies * padded
    flat = owners * chunk
    slots = owners * padded
    anywhere = pl.BlockSpec(memory_space=pl.ANY)
    vmem = pl.BlockSpec(memory_space=pltpu.VMEM)
    dma = pltpu.SemaphoreType.DMA
    blocks = (2, owners, chunk, width)
    back, places = pl.pallas_call(
        functools.partial(kernel, live, padded),
        out_shape=(
            jax.ShapeDtypeStruct(blocks, BF16),
            jax.ShapeDtypeStruct((energies, block, flat), BF16),
        ),
        in_specs=[anywhere] * 5,
        out_specs=(vmem, vmem),
        scratch_shapes=[
            pltpu.VMEM(retarded.shape, BF16),
            pltpu.VMEM(injection.shape, BF16),
            pltpu.VMEM(screened.shape, BF16),
            pltpu.VMEM((1, block), pattern.dtype),
            pltpu.VMEM(tables.shape, BF16),
            pltpu.VMEM((2, 2, energies, block, width), BF16),
            pltpu.VMEM((3, energies, 2 * block, width), BF16),
            pltpu.VMEM((3, energies, slots, width), BF16),
            pltpu.VMEM((2, energies, slots, width), F32),
            pltpu.VMEM((2, flat, width), F32),
            pltpu.VMEM((owners, 2, chunk, width), BF16),
            pltpu.VMEM((owners, 2, chunk, width), BF16),
            pltpu.VMEM(blocks, BF16),
            pltpu.VMEM(blocks, BF16),
            pltpu.VMEM(blocks, BF16),
            dma((5,)),
            dma((2, 2)),
            dma((2, 2)),
            dma,
            dma,
            dma((2,)),
            dma((2,)),
            dma((2,)),
            dma((2,)),
            dma((2,)),
        ],
        compiler_params=pltpu.CompilerParams(
            collective_id=0, has_side_effects=True, vmem_limit_bytes=53 * 1024 * 1024
        ),
    )(
        retarded,
        injection,
        screened,
        pattern.reshape(1, -1),
        jnp.asarray(tables),
    )
    return pl.pallas_call(
        expand,
        out_shape=jax.ShapeDtypeStruct(screened.shape, BF16),
        in_specs=[vmem, vmem],
        out_specs=vmem,
        compiler_params=pltpu.CompilerParams(vmem_limit_bytes=32 * 1024 * 1024),
    )(back, places)


def solution(mesh):
    placed = (
        P("energy", None, "slab", None),
        P("energy", None, "slab", None),
        P("energy", None, "slab", None),
        P("slab"),
    )
    return jax.shard_map(
        local,
        mesh=mesh,
        in_specs=placed,
        out_specs=P("energy", None, "slab", None),
        check_vma=False,
    )
```

```python
import functools
import math

import jax
import jax.numpy as jnp
import numpy as np
from jax import lax
from jax.experimental import pallas as pl
from jax.experimental.pallas import tpu as pltpu
from jax.sharding import PartitionSpec as P

MESH = pl.DeviceIdType.MESH
F32 = jnp.float32
BF16 = jnp.bfloat16


def dot(a, b):
    return jnp.dot(a, b, preferred_element_type=F32)


def dot_nt(a, b):
    return lax.dot_general(a, b, (((1,), (1,)), ((), ())), preferred_element_type=F32)


def times_i(x):
    half = x.shape[-1] // 2
    lane = lax.broadcasted_iota(jnp.int32, x.shape, 1)
    turned = pltpu.roll(x, half, 1)
    return jnp.where(lane < half, -turned, turned)


def complex_times(x, y):
    half = x.shape[-1] // 2
    first = lax.broadcasted_iota(jnp.int32, x.shape, 1) < half
    turned = pltpu.roll(y, half, 1)
    return x * jnp.where(first, y, turned) + times_i(x) * jnp.where(first, turned, y)


def kernel(
    live, padded,
    retarded, injection, screened, pattern, tables,
    back, places,
    ret_v, inj_v, scr_v, pat_v, tab_v,
    halo, row_wide, row_live, total, screen_hat,
    s_send, s_recv, g_send, g_recv, c_send,
    load_sem, halo_out, halo_in, s_out, s_in, g_out, g_in, c_out, c_in, own_sem,
):
    owners = lax.axis_size("energy")
    slabs = lax.axis_size("slab")
    me = lax.axis_index("energy")
    slab = lax.axis_index("slab")
    has_left = slab > 0
    has_right = slab < slabs - 1
    energies, _, block, width = ret_v.shape
    chunk = s_send.shape[2]
    per_energy = chunk // energies
    flat = owners * chunk
    count = owners * energies

    share = -(-live // owners)
    loads = [
        pltpu.make_async_copy(source, target, load_sem.at[at])
        for at, (source, target) in enumerate(
            [
                (pattern, pat_v),
                (screened, scr_v),
                (retarded, ret_v),
                (injection, inj_v),
                (tables, tab_v),
            ]
        )
    ]
    for load in loads:
        load.start()

    barrier = pltpu.get_barrier_semaphore()

    def greet(step, carry):
        peer = lax.rem(me + step, owners)
        pl.semaphore_signal(barrier, inc=1, device_id={"energy": peer}, device_id_type=MESH)
        return carry

    lax.fori_loop(1, owners, greet, 0)

    @pl.when(has_left)
    def _():
        pl.semaphore_signal(barrier, inc=1, device_id={"slab": slab - 1}, device_id_type=MESH)

    @pl.when(has_right)
    def _():
        pl.semaphore_signal(barrier, inc=1, device_id={"slab": slab + 1}, device_id_type=MESH)

    def spread(source, target, out_sem, in_sem):
        def send(step, carry):
            peer = lax.rem(me + step, owners)
            pltpu.make_async_remote_copy(
                src_ref=source.at[peer],
                dst_ref=target.at[me],
                send_sem=out_sem,
                recv_sem=in_sem,
                device_id={"energy": peer},
                device_id_type=MESH,
            ).start()
            return carry

        lax.fori_loop(1, owners, send, 0)

    def wait_all(buffer, sem):
        rest = buffer.at[pl.ds(0, owners - 1)]
        pltpu.make_async_copy(rest, rest, sem).wait()

    pl.semaphore_wait(
        barrier, owners - 1 + has_left.astype(jnp.int32) + has_right.astype(jnp.int32)
    )

    def halo_copy(side, kind):
        return pltpu.make_async_remote_copy(
            src_ref=injection.at[:, kind],
            dst_ref=halo.at[side, kind],
            send_sem=halo_out.at[side, kind],
            recv_sem=halo_in.at[side, kind],
            device_id={"slab": slab + 1 - 2 * side},
            device_id_type=MESH,
        )

    def send_halo(kind):
        @pl.when(has_right)
        def _():
            halo_copy(0, kind).start()

        @pl.when(has_left)
        def _():
            halo_copy(1, kind).start()

    def take_halo(kind):
        @pl.when(has_left)
        def _():
            halo_copy(0, kind).wait_recv()

        @pl.when(has_right)
        def _():
            halo_copy(1, kind).wait_recv()

    send_halo(0)
    send_halo(1)

    loads[0].wait()
    pattern_row = pat_v[...].astype(F32)
    down = lax.broadcasted_iota(jnp.int32, (block, block), 0)
    across = lax.broadcasted_iota(jnp.int32, (block, block), 1)
    pattern_col = jnp.sum(jnp.where(down == across, pattern_row, 0.0), 1, keepdims=True)
    rank_col = jnp.sum(jnp.where(across < down, pattern_row, 0.0), 1, keepdims=True)
    rank_row = jnp.sum(jnp.where(down < across, pattern_col, 0.0), 0, keepdims=True)
    key_col = jnp.where(pattern_col > 0.5, rank_col, -1.0)
    key_row = jnp.where(pattern_row > 0.5, rank_row, -1.0)

    def one_hot(left, right):
        return jnp.where(left == right, 1.0, 0.0).astype(BF16)

    def wanted(shape, axis, size, energy):
        at = lax.broadcasted_iota(jnp.int32, shape, axis).astype(F32)
        owner = jnp.floor((at + 0.5) * (1.0 / size))
        inside = at - owner * size - energy * padded
        row = owner * share + inside
        return jnp.where((inside >= 0) & (inside < share) & (row < live), row, -2.0)

    picks = [one_hot(wanted((flat, 1), 0, chunk, e), key_row) for e in range(energies)]
    loads[1].wait()
    for kind in range(2):
        picked = sum(dot(picks[e], scr_v[e, kind]) for e in range(energies))
        s_send[:, kind] = picked.astype(BF16).reshape(owners, chunk, width)

    spread(s_send, s_recv, s_out, s_in)
    s_recv[me] = s_send[me]

    pick_rows = one_hot(wanted((owners * padded, 1), 0, padded, 0), key_row)

    def widen(x):
        return times_i(x.astype(F32)).astype(BF16)

    def prepare(offset):
        for e in range(energies):
            rows = ret_v[e, offset]
            row_wide[offset, e, :block] = rows
            row_wide[offset, e, block:] = widen(rows)
            row_live[offset, e] = dot(pick_rows, rows).astype(BF16)

    def term(offset, e, inject):
        expanded = jnp.concatenate([inject, widen(inject)], 0)
        left = dot(row_live[offset, e], expanded).astype(BF16)
        return dot_nt(left, row_wide[offset, e])

    loads[2].wait()
    loads[3].wait()
    prepare(1)

    @pl.when(has_left)
    def _():
        prepare(0)

    @pl.when(has_right)
    def _():
        prepare(2)

    for kind in range(2):
        for e in range(energies):
            total[kind, e] = term(1, e, inj_v[e, kind])

    def green(kind):
        @pl.when(has_left)
        def _():
            for e in range(energies):
                total[kind, e] += term(0, e, halo[0, kind, e])

        @pl.when(has_right)
        def _():
            for e in range(energies):
                total[kind, e] += term(2, e, halo[1, kind, e])

        parts = [total[kind, e].reshape(owners, per_energy, width) for e in range(energies)]
        g_send[kind] = jnp.concatenate(parts, 1).astype(BF16)
        spread(g_send.at[kind], g_recv.at[kind], g_out.at[kind], g_in.at[kind])
        g_recv[kind, me] = g_send[kind, me]

    def transform(pieces):
        return dot(tab_v[:, : flat * len(pieces)], jnp.concatenate(pieces, 0))

    def forward(values):
        turned = widen(values)
        return transform([values, turned, values, turned])

    factor = 1.0 / (count * math.sqrt(count))

    def convolve(kind):
        wait_all(g_recv.at[kind], g_in.at[kind])
        green_hat = forward(g_recv[kind].reshape(flat, width))
        product = complex_times(green_hat, screen_hat[kind])
        turned = times_i(product)
        high, turned_high = product.astype(BF16), turned.astype(BF16)
        low = (product - high.astype(F32)).astype(BF16)
        turned_low = (turned - turned_high.astype(F32)).astype(BF16)
        sigma = transform([turned_high, high, turned_high, high, turned_low, low])
        c_send[kind] = (sigma * factor).astype(BF16).reshape(owners, chunk, width)
        spread(c_send.at[kind], back.at[kind], c_out.at[kind], c_in.at[kind])

    def keep_own(kind):
        own = pltpu.make_async_copy(c_send.at[kind, me], back.at[kind, me], own_sem.at[kind])
        own.start()
        return own

    take_halo(0)
    green(0)
    loads[4].wait()
    wait_all(s_recv, s_in)
    for kind in range(2):
        screen_hat[kind] = forward(s_recv[:, kind].reshape(flat, width))
    take_halo(1)
    green(1)
    convolve(0)
    convolve(1)
    owns = [keep_own(0), keep_own(1)]
    for e in range(energies):
        places[e] = one_hot(key_col, wanted((1, flat), 1, chunk, e))

    for kind in range(2):
        @pl.when(has_right)
        def _():
            halo_copy(0, kind).wait_send()

        @pl.when(has_left)
        def _():
            halo_copy(1, kind).wait_send()

    wait_all(s_send, s_out)
    for kind in range(2):
        wait_all(g_send.at[kind], g_out.at[kind])
        wait_all(c_send.at[kind], c_out.at[kind])
        wait_all(back.at[kind], c_in.at[kind])
        owns[kind].wait()


def expand(back, places, result):
    energies, kinds = result.shape[:2]
    for kind in range(kinds):
        rows = back[kind].reshape(-1, back.shape[-1])
        for e in range(energies):
            result[e, kind] = dot(places[e], rows).astype(BF16)


def transform_tables(count, padded):
    index = np.arange(count)
    angle = 2.0 * np.pi / count * (index[:, None] * index[None, :] % count)
    tables = np.stack([np.cos(angle), -np.sin(angle)]).astype(np.float32)
    high = tables.astype(jnp.bfloat16).astype(np.float32)
    low = (tables - high).astype(jnp.bfloat16).astype(np.float32)
    eye = np.eye(padded, dtype=np.float32)
    wide = [np.kron(table, eye) for table in (*high, *low, *high)]
    return np.concatenate(wide, 1).astype(jnp.bfloat16)


def local(retarded, injection, screened, pattern):
    energies, _, block, width = retarded.shape
    owners = lax.axis_size("energy")
    live = block * 2 // 3
    padded = -(-live // (owners * 8)) * 8
    while energies * padded % 16:
        padded += 8
    tables = transform_tables(owners * energies, padded)
    chunk = energies * padded
    flat = owners * chunk
    slots = owners * padded
    anywhere = pl.BlockSpec(memory_space=pl.ANY)
    vmem = pl.BlockSpec(memory_space=pltpu.VMEM)
    dma = pltpu.SemaphoreType.DMA
    blocks = (2, owners, chunk, width)
    back, places = pl.pallas_call(
        functools.partial(kernel, live, padded),
        out_shape=(
            jax.ShapeDtypeStruct(blocks, BF16),
            jax.ShapeDtypeStruct((energies, block, flat), BF16),
        ),
        in_specs=[anywhere] * 5,
        out_specs=(vmem, vmem),
        scratch_shapes=[
            pltpu.VMEM(retarded.shape, BF16),
            pltpu.VMEM(injection.shape, BF16),
            pltpu.VMEM(screened.shape, BF16),
            pltpu.VMEM((1, block), pattern.dtype),
            pltpu.VMEM(tables.shape, BF16),
            pltpu.VMEM((2, 2, energies, block, width), BF16),
            pltpu.VMEM((3, energies, 2 * block, width), BF16),
            pltpu.VMEM((3, energies, slots, width), BF16),
            pltpu.VMEM((2, energies, slots, width), F32),
            pltpu.VMEM((2, flat, width), F32),
            pltpu.VMEM((owners, 2, chunk, width), BF16),
            pltpu.VMEM((owners, 2, chunk, width), BF16),
            pltpu.VMEM(blocks, BF16),
            pltpu.VMEM(blocks, BF16),
            pltpu.VMEM(blocks, BF16),
            dma((5,)),
            dma((2, 2)),
            dma((2, 2)),
            dma,
            dma,
            dma((2,)),
            dma((2,)),
            dma((2,)),
            dma((2,)),
            dma((2,)),
        ],
        compiler_params=pltpu.CompilerParams(
            collective_id=0, has_side_effects=True, vmem_limit_bytes=53 * 1024 * 1024
        ),
    )(
        retarded,
        injection,
        screened,
        pattern.reshape(1, -1),
        jnp.asarray(tables),
    )
    return pl.pallas_call(
        expand,
        out_shape=jax.ShapeDtypeStruct(screened.shape, BF16),
        in_specs=[vmem, vmem],
        out_specs=vmem,
        compiler_params=pltpu.CompilerParams(vmem_limit_bytes=32 * 1024 * 1024),
    )(back, places)


def solution(mesh):
    placed = (
        P("energy", None, "slab", None),
        P("energy", None, "slab", None),
        P("energy", None, "slab", None),
        P("slab"),
    )
    return jax.shard_map(
        local,
        mesh=mesh,
        in_specs=placed,
        out_specs=P("energy", None, "slab", None),
        check_vma=False,
    )
```

```python
import functools
import math

import jax
import jax.numpy as jnp
import numpy as np
from jax import lax
from jax.experimental import pallas as pl
from jax.experimental.pallas import tpu as pltpu
from jax.sharding import PartitionSpec as P

MESH = pl.DeviceIdType.MESH
F32 = jnp.float32
BF16 = jnp.bfloat16


def dot(a, b):
    return jnp.dot(a, b, preferred_element_type=F32)


def dot_nt(a, b):
    return lax.dot_general(a, b, (((1,), (1,)), ((), ())), preferred_element_type=F32)


def times_i(x):
    half = x.shape[-1] // 2
    lane = lax.broadcasted_iota(jnp.int32, x.shape, 1)
    turned = pltpu.roll(x, half, 1)
    return jnp.where(lane < half, -turned, turned)


def complex_times(x, y):
    half = x.shape[-1] // 2
    first = lax.broadcasted_iota(jnp.int32, x.shape, 1) < half
    turned = pltpu.roll(y, half, 1)
    return x * jnp.where(first, y, turned) + times_i(x) * jnp.where(first, turned, y)


def kernel(
    live, padded,
    retarded, injection, screened, pattern, tables,
    back, places,
    ret_v, inj_v, scr_v, pat_v, tab_v,
    halo, row_wide, row_live, total, screen_hat,
    s_send, s_recv, g_send, g_recv, c_send,
    load_sem, halo_out, halo_in, s_out, s_in, g_out, g_in, c_out, c_in, own_sem,
):
    owners = lax.axis_size("energy")
    slabs = lax.axis_size("slab")
    me = lax.axis_index("energy")
    slab = lax.axis_index("slab")
    has_left = slab > 0
    has_right = slab < slabs - 1
    energies, _, block, width = ret_v.shape
    chunk = s_send.shape[2]
    per_energy = chunk // energies
    flat = owners * chunk
    count = owners * energies

    share = -(-live // owners)
    loads = [
        pltpu.make_async_copy(source, target, load_sem.at[at])
        for at, (source, target) in enumerate(
            [
                (pattern, pat_v),
                (screened, scr_v),
                (retarded, ret_v),
                (injection, inj_v),
                (tables, tab_v),
            ]
        )
    ]
    for load in loads:
        load.start()

    barrier = pltpu.get_barrier_semaphore()

    def greet(step, carry):
        peer = lax.rem(me + step, owners)
        pl.semaphore_signal(barrier, inc=1, device_id={"energy": peer}, device_id_type=MESH)
        return carry

    lax.fori_loop(1, owners, greet, 0)

    @pl.when(has_left)
    def _():
        pl.semaphore_signal(barrier, inc=1, device_id={"slab": slab - 1}, device_id_type=MESH)

    @pl.when(has_right)
    def _():
        pl.semaphore_signal(barrier, inc=1, device_id={"slab": slab + 1}, device_id_type=MESH)

    def spread(source, target, out_sem, in_sem):
        def send(step, carry):
            peer = lax.rem(me + step, owners)
            pltpu.make_async_remote_copy(
                src_ref=source.at[peer],
                dst_ref=target.at[me],
                send_sem=out_sem,
                recv_sem=in_sem,
                device_id={"energy": peer},
                device_id_type=MESH,
            ).start()
            return carry

        lax.fori_loop(1, owners, send, 0)

    def wait_all(buffer, sem):
        rest = buffer.at[pl.ds(0, owners - 1)]
        pltpu.make_async_copy(rest, rest, sem).wait()

    pl.semaphore_wait(
        barrier, owners - 1 + has_left.astype(jnp.int32) + has_right.astype(jnp.int32)
    )

    def halo_copy(side, kind, e):
        return pltpu.make_async_remote_copy(
            src_ref=injection.at[e, kind],
            dst_ref=halo.at[side, kind, e],
            send_sem=halo_out.at[side, kind, e],
            recv_sem=halo_in.at[side, kind, e],
            device_id={"slab": slab + 1 - 2 * side},
            device_id_type=MESH,
        )

    pieces = [(kind, e) for kind in range(2) for e in range(energies)]
    for piece in pieces:
        @pl.when(has_right)
        def _():
            halo_copy(0, *piece).start()

        @pl.when(has_left)
        def _():
            halo_copy(1, *piece).start()

    loads[0].wait()
    pattern_row = pat_v[...].astype(F32)
    down = lax.broadcasted_iota(jnp.int32, (block, block), 0)
    across = lax.broadcasted_iota(jnp.int32, (block, block), 1)
    pattern_col = jnp.sum(jnp.where(down == across, pattern_row, 0.0), 1, keepdims=True)
    rank_col = jnp.sum(jnp.where(across < down, pattern_row, 0.0), 1, keepdims=True)
    rank_row = jnp.sum(jnp.where(down < across, pattern_col, 0.0), 0, keepdims=True)
    key_col = jnp.where(pattern_col > 0.5, rank_col, -1.0)
    key_row = jnp.where(pattern_row > 0.5, rank_row, -1.0)

    def one_hot(left, right):
        return jnp.where(left == right, 1.0, 0.0).astype(BF16)

    def wanted(shape, axis, size, energy):
        at = lax.broadcasted_iota(jnp.int32, shape, axis).astype(F32)
        owner = jnp.floor((at + 0.5) * (1.0 / size))
        inside = at - owner * size - energy * padded
        row = owner * share + inside
        return jnp.where((inside >= 0) & (inside < share) & (row < live), row, -2.0)

    picks = [one_hot(wanted((flat, 1), 0, chunk, e), key_row) for e in range(energies)]
    loads[1].wait()
    for kind in range(2):
        picked = sum(dot(picks[e], scr_v[e, kind]) for e in range(energies))
        s_send[:, kind] = picked.astype(BF16).reshape(owners, chunk, width)

    spread(s_send, s_recv, s_out, s_in)
    s_recv[me] = s_send[me]

    pick_rows = one_hot(wanted((owners * padded, 1), 0, padded, 0), key_row)

    def widen(x):
        return times_i(x.astype(F32)).astype(BF16)

    def prepare(offset):
        for e in range(energies):
            rows = ret_v[e, offset]
            row_wide[offset, e, :block] = rows
            row_wide[offset, e, block:] = widen(rows)
            row_live[offset, e] = dot(pick_rows, rows).astype(BF16)

    def term(offset, e, inject):
        expanded = jnp.concatenate([inject, widen(inject)], 0)
        left = dot(row_live[offset, e], expanded).astype(BF16)
        return dot_nt(left, row_wide[offset, e])

    loads[2].wait()
    loads[3].wait()
    prepare(1)

    @pl.when(has_left)
    def _():
        prepare(0)

    @pl.when(has_right)
    def _():
        prepare(2)

    for kind in range(2):
        for e in range(energies):
            total[kind, e] = term(1, e, inj_v[e, kind])

    def green(kind, e):
        @pl.when(has_left)
        def _():
            halo_copy(0, kind, e).wait_recv()
            total[kind, e] += term(0, e, halo[0, kind, e])

        @pl.when(has_right)
        def _():
            halo_copy(1, kind, e).wait_recv()
            total[kind, e] += term(2, e, halo[1, kind, e])

        at = (kind, e)
        g_send[kind, e] = total[kind, e].reshape(owners, per_energy, width).astype(BF16)
        spread(g_send.at[at], g_recv.at[at], g_out.at[at], g_in.at[at])
        g_recv[kind, e, me] = g_send[kind, e, me]

    def green_rows(kind):
        parts = []
        for e in range(energies):
            wait_all(g_recv.at[kind, e], g_in.at[kind, e])
            parts.append(g_recv[kind, e].astype(F32))
        return jnp.concatenate(parts, 1).reshape(flat, width).astype(BF16)

    def transform(pieces):
        return dot(tab_v[:, : flat * len(pieces)], jnp.concatenate(pieces, 0))

    def forward(values):
        turned = widen(values)
        return transform([values, turned, values, turned])

    factor = 1.0 / (count * math.sqrt(count))

    def convolve(kind):
        green_hat = forward(green_rows(kind))
        product = complex_times(green_hat, screen_hat[kind])
        turned = times_i(product)
        high, turned_high = product.astype(BF16), turned.astype(BF16)
        low = (product - high.astype(F32)).astype(BF16)
        turned_low = (turned - turned_high.astype(F32)).astype(BF16)
        sigma = transform([turned_high, high, turned_high, high, turned_low, low])
        c_send[kind] = (sigma * factor).astype(BF16).reshape(owners, chunk, width)
        spread(c_send.at[kind], back.at[kind], c_out.at[kind], c_in.at[kind])

    def keep_own(kind):
        own = pltpu.make_async_copy(c_send.at[kind, me], back.at[kind, me], own_sem.at[kind])
        own.start()
        return own

    for e in range(energies):
        green(0, e)
    loads[4].wait()
    wait_all(s_recv, s_in)
    for kind in range(2):
        screen_hat[kind] = forward(s_recv[:, kind].reshape(flat, width))
    for e in range(energies):
        green(1, e)
    convolve(0)
    convolve(1)
    owns = [keep_own(0), keep_own(1)]
    for e in range(energies):
        places[e] = one_hot(key_col, wanted((1, flat), 1, chunk, e))

    for piece in pieces:
        @pl.when(has_right)
        def _():
            halo_copy(0, *piece).wait_send()

        @pl.when(has_left)
        def _():
            halo_copy(1, *piece).wait_send()

        wait_all(g_send.at[piece], g_out.at[piece])

    wait_all(s_send, s_out)
    for kind in range(2):
        wait_all(c_send.at[kind], c_out.at[kind])
        wait_all(back.at[kind], c_in.at[kind])
        owns[kind].wait()


def expand(back, places, result):
    energies, kinds = result.shape[:2]
    for kind in range(kinds):
        rows = back[kind].reshape(-1, back.shape[-1])
        for e in range(energies):
            result[e, kind] = dot(places[e], rows).astype(BF16)


def transform_tables(count, padded):
    index = np.arange(count)
    angle = 2.0 * np.pi / count * (index[:, None] * index[None, :] % count)
    tables = np.stack([np.cos(angle), -np.sin(angle)]).astype(np.float32)
    high = tables.astype(jnp.bfloat16).astype(np.float32)
    low = (tables - high).astype(jnp.bfloat16).astype(np.float32)
    eye = np.eye(padded, dtype=np.float32)
    wide = [np.kron(table, eye) for table in (*high, *low, *high)]
    return np.concatenate(wide, 1).astype(jnp.bfloat16)


def local(retarded, injection, screened, pattern):
    energies, _, block, width = retarded.shape
    owners = lax.axis_size("energy")
    live = block * 2 // 3
    padded = -(-live // (owners * 8)) * 8
    while energies * padded % 16:
        padded += 8
    tables = transform_tables(owners * energies, padded)
    chunk = energies * padded
    flat = owners * chunk
    slots = owners * padded
    anywhere = pl.BlockSpec(memory_space=pl.ANY)
    vmem = pl.BlockSpec(memory_space=pltpu.VMEM)
    dma = pltpu.SemaphoreType.DMA
    blocks = (2, owners, chunk, width)
    back, places = pl.pallas_call(
        functools.partial(kernel, live, padded),
        out_shape=(
            jax.ShapeDtypeStruct(blocks, BF16),
            jax.ShapeDtypeStruct((energies, block, flat), BF16),
        ),
        in_specs=[anywhere] * 5,
        out_specs=(vmem, vmem),
        scratch_shapes=[
            pltpu.VMEM(retarded.shape, BF16),
            pltpu.VMEM(injection.shape, BF16),
            pltpu.VMEM(screened.shape, BF16),
            pltpu.VMEM((1, block), pattern.dtype),
            pltpu.VMEM(tables.shape, BF16),
            pltpu.VMEM((2, 2, energies, block, width), BF16),
            pltpu.VMEM((3, energies, 2 * block, width), BF16),
            pltpu.VMEM((3, energies, slots, width), BF16),
            pltpu.VMEM((2, energies, slots, width), F32),
            pltpu.VMEM((2, flat, width), F32),
            pltpu.VMEM((owners, 2, chunk, width), BF16),
            pltpu.VMEM((owners, 2, chunk, width), BF16),
            pltpu.VMEM((2, energies, owners, padded, width), BF16),
            pltpu.VMEM((2, energies, owners, padded, width), BF16),
            pltpu.VMEM(blocks, BF16),
            dma((5,)),
            dma((2, 2, energies)),
            dma((2, 2, energies)),
            dma,
            dma,
            dma((2, energies)),
            dma((2, energies)),
            dma((2,)),
            dma((2,)),
            dma((2,)),
        ],
        compiler_params=pltpu.CompilerParams(
            collective_id=0, has_side_effects=True, vmem_limit_bytes=53 * 1024 * 1024
        ),
    )(
        retarded,
        injection,
        screened,
        pattern.reshape(1, -1),
        jnp.asarray(tables),
    )
    return pl.pallas_call(
        expand,
        out_shape=jax.ShapeDtypeStruct(screened.shape, BF16),
        in_specs=[vmem, vmem],
        out_specs=vmem,
        compiler_params=pltpu.CompilerParams(vmem_limit_bytes=32 * 1024 * 1024),
    )(back, places)


def solution(mesh):
    placed = (
        P("energy", None, "slab", None),
        P("energy", None, "slab", None),
        P("energy", None, "slab", None),
        P("slab"),
    )
    return jax.shard_map(
        local,
        mesh=mesh,
        in_specs=placed,
        out_specs=P("energy", None, "slab", None),
        check_vma=False,
    )
```

```python
import functools
import math

import jax
import jax.numpy as jnp
import numpy as np
from jax import lax
from jax.experimental import pallas as pl
from jax.experimental.pallas import tpu as pltpu
from jax.sharding import PartitionSpec as P

MESH = pl.DeviceIdType.MESH
F32 = jnp.float32
BF16 = jnp.bfloat16


def dot(a, b):
    return jnp.dot(a, b, preferred_element_type=F32)


def dot_nt(a, b):
    return lax.dot_general(a, b, (((1,), (1,)), ((), ())), preferred_element_type=F32)


def times_i(x):
    half = x.shape[-1] // 2
    lane = lax.broadcasted_iota(jnp.int32, x.shape, 1)
    turned = pltpu.roll(x, half, 1)
    return jnp.where(lane < half, -turned, turned)


def complex_times(x, y):
    half = x.shape[-1] // 2
    first = lax.broadcasted_iota(jnp.int32, x.shape, 1) < half
    turned = pltpu.roll(y, half, 1)
    return x * jnp.where(first, y, turned) + times_i(x) * jnp.where(first, turned, y)


def kernel(
    live, padded,
    retarded, injection, screened, pattern, tables,
    back, places,
    ret_v, inj_v, scr_v, pat_v, tab_v,
    halo, row_wide, row_live, total, screen_hat,
    s_send, s_recv, g_send, g_recv, c_send,
    load_sem, halo_out, halo_in, s_out, s_in, g_out, g_in, c_out, c_in, own_sem,
):
    owners = lax.axis_size("energy")
    slabs = lax.axis_size("slab")
    me = lax.axis_index("energy")
    slab = lax.axis_index("slab")
    has_left = slab > 0
    has_right = slab < slabs - 1
    energies, _, block, width = ret_v.shape
    chunk = s_send.shape[2]
    per_energy = chunk // energies
    flat = owners * chunk
    count = owners * energies

    share = -(-live // owners)
    loads = [
        pltpu.make_async_copy(source, target, load_sem.at[at])
        for at, (source, target) in enumerate(
            [
                (pattern, pat_v),
                (screened, scr_v),
                (retarded, ret_v),
                (injection, inj_v),
                (tables, tab_v),
            ]
        )
    ]
    for load in loads:
        load.start()

    barrier = pltpu.get_barrier_semaphore()

    def greet(step, carry):
        peer = lax.rem(me + step, owners)
        pl.semaphore_signal(barrier, inc=1, device_id={"energy": peer}, device_id_type=MESH)
        return carry

    lax.fori_loop(1, owners, greet, 0)

    @pl.when(has_left)
    def _():
        pl.semaphore_signal(barrier, inc=1, device_id={"slab": slab - 1}, device_id_type=MESH)

    @pl.when(has_right)
    def _():
        pl.semaphore_signal(barrier, inc=1, device_id={"slab": slab + 1}, device_id_type=MESH)

    def spread(source, target, out_sem, in_sem):
        def send(step, carry):
            peer = lax.rem(me + step, owners)
            pltpu.make_async_remote_copy(
                src_ref=source.at[peer],
                dst_ref=target.at[me],
                send_sem=out_sem,
                recv_sem=in_sem,
                device_id={"energy": peer},
                device_id_type=MESH,
            ).start()
            return carry

        lax.fori_loop(1, owners, send, 0)

    def wait_all(buffer, sem):
        rest = buffer.at[pl.ds(0, owners - 1)]
        pltpu.make_async_copy(rest, rest, sem).wait()

    pl.semaphore_wait(
        barrier, owners - 1 + has_left.astype(jnp.int32) + has_right.astype(jnp.int32)
    )

    def halo_copy(side, kind, e):
        return pltpu.make_async_remote_copy(
            src_ref=injection.at[e, kind],
            dst_ref=halo.at[side, kind, e],
            send_sem=halo_out.at[side, kind, e],
            recv_sem=halo_in.at[side, kind, e],
            device_id={"slab": slab + 1 - 2 * side},
            device_id_type=MESH,
        )

    pieces = [(kind, e) for kind in range(2) for e in range(energies)]
    for piece in pieces:
        @pl.when(has_right)
        def _():
            halo_copy(0, *piece).start()

        @pl.when(has_left)
        def _():
            halo_copy(1, *piece).start()

    loads[0].wait()
    pattern_row = pat_v[...].astype(F32)
    down = lax.broadcasted_iota(jnp.int32, (block, block), 0)
    across = lax.broadcasted_iota(jnp.int32, (block, block), 1)
    pattern_col = jnp.sum(jnp.where(down == across, pattern_row, 0.0), 1, keepdims=True)
    rank_col = jnp.sum(jnp.where(across < down, pattern_row, 0.0), 1, keepdims=True)
    rank_row = jnp.sum(jnp.where(down < across, pattern_col, 0.0), 0, keepdims=True)
    key_col = jnp.where(pattern_col > 0.5, rank_col, -1.0)
    key_row = jnp.where(pattern_row > 0.5, rank_row, -1.0)

    def one_hot(left, right):
        return jnp.where(left == right, 1.0, 0.0).astype(BF16)

    def wanted(shape, axis, size, energy):
        at = lax.broadcasted_iota(jnp.int32, shape, axis).astype(F32)
        owner = jnp.floor((at + 0.5) * (1.0 / size))
        inside = at - owner * size - energy * padded
        row = owner * share + inside
        return jnp.where((inside >= 0) & (inside < share) & (row < live), row, -2.0)

    picks = [one_hot(wanted((flat, 1), 0, chunk, e), key_row) for e in range(energies)]
    loads[1].wait()
    for kind in range(2):
        picked = sum(dot(picks[e], scr_v[e, kind]) for e in range(energies))
        s_send[:, kind] = picked.astype(BF16).reshape(owners, chunk, width)

    spread(s_send, s_recv, s_out, s_in)
    s_recv[me] = s_send[me]

    pick_rows = one_hot(wanted((owners * padded, 1), 0, padded, 0), key_row)

    def widen(x):
        return times_i(x.astype(F32)).astype(BF16)

    def prepare(offset):
        for e in range(energies):
            rows = ret_v[e, offset]
            row_wide[offset, e, :block] = rows
            row_wide[offset, e, block:] = widen(rows)
            row_live[offset, e] = dot(pick_rows, rows).astype(BF16)

    def term(offset, e, inject):
        expanded = jnp.concatenate([inject, widen(inject)], 0)
        left = dot(row_live[offset, e], expanded).astype(BF16)
        return dot_nt(left, row_wide[offset, e])

    loads[2].wait()
    loads[3].wait()
    prepare(1)

    @pl.when(has_left)
    def _():
        prepare(0)

    @pl.when(has_right)
    def _():
        prepare(2)

    for kind in range(2):
        for e in range(energies):
            total[kind, e] = term(1, e, inj_v[e, kind])

    def green(kind, e):
        @pl.when(has_left)
        def _():
            halo_copy(0, kind, e).wait_recv()
            total[kind, e] += term(0, e, halo[0, kind, e])

        @pl.when(has_right)
        def _():
            halo_copy(1, kind, e).wait_recv()
            total[kind, e] += term(2, e, halo[1, kind, e])

        at = (kind, e)
        g_send[kind, e] = total[kind, e].reshape(owners, per_energy, width).astype(BF16)
        spread(g_send.at[at], g_recv.at[at], g_out.at[at], g_in.at[at])
        g_recv[kind, e, me] = g_send[kind, e, me]

    def green_rows(kind):
        parts = []
        for e in range(energies):
            wait_all(g_recv.at[kind, e], g_in.at[kind, e])
            parts.append(g_recv[kind, e].astype(F32))
        return jnp.concatenate(parts, 1).reshape(flat, width).astype(BF16)

    def transform(pieces):
        return dot(tab_v[:, : flat * len(pieces)], jnp.concatenate(pieces, 0))

    def forward(values):
        turned = widen(values)
        return transform([values, turned, values, turned])

    factor = 1.0 / (count * math.sqrt(count))

    def convolve(kind):
        green_hat = forward(green_rows(kind))
        product = complex_times(green_hat, screen_hat[kind])
        turned = times_i(product)
        high, turned_high = product.astype(BF16), turned.astype(BF16)
        low = (product - high.astype(F32)).astype(BF16)
        turned_low = (turned - turned_high.astype(F32)).astype(BF16)
        sigma = transform([turned_high, high, turned_high, high, turned_low, low])
        c_send[kind] = (sigma * factor).astype(BF16).reshape(owners, chunk, width)
        spread(c_send.at[kind], back.at[kind], c_out.at[kind], c_in.at[kind])

    def keep_own(kind):
        own = pltpu.make_async_copy(c_send.at[kind, me], back.at[kind, me], own_sem.at[kind])
        own.start()
        return own

    for e in range(energies):
        green(0, e)
    loads[4].wait()
    wait_all(s_recv, s_in)
    for kind in range(2):
        screen_hat[kind] = forward(s_recv[:, kind].reshape(flat, width))
    for e in range(energies - 1):
        green(1, e)
    convolve(0)
    green(1, energies - 1)
    convolve(1)
    owns = [keep_own(0), keep_own(1)]
    for e in range(energies):
        places[e] = one_hot(key_col, wanted((1, flat), 1, chunk, e))

    for piece in pieces:
        @pl.when(has_right)
        def _():
            halo_copy(0, *piece).wait_send()

        @pl.when(has_left)
        def _():
            halo_copy(1, *piece).wait_send()

        wait_all(g_send.at[piece], g_out.at[piece])

    wait_all(s_send, s_out)
    for kind in range(2):
        wait_all(c_send.at[kind], c_out.at[kind])
        wait_all(back.at[kind], c_in.at[kind])
        owns[kind].wait()


def expand(back, places, result):
    energies, kinds = result.shape[:2]
    for kind in range(kinds):
        rows = back[kind].reshape(-1, back.shape[-1])
        for e in range(energies):
            result[e, kind] = dot(places[e], rows).astype(BF16)


def transform_tables(count, padded):
    index = np.arange(count)
    angle = 2.0 * np.pi / count * (index[:, None] * index[None, :] % count)
    tables = np.stack([np.cos(angle), -np.sin(angle)]).astype(np.float32)
    high = tables.astype(jnp.bfloat16).astype(np.float32)
    low = (tables - high).astype(jnp.bfloat16).astype(np.float32)
    eye = np.eye(padded, dtype=np.float32)
    wide = [np.kron(table, eye) for table in (*high, *low, *high)]
    return np.concatenate(wide, 1).astype(jnp.bfloat16)


def local(retarded, injection, screened, pattern):
    energies, _, block, width = retarded.shape
    owners = lax.axis_size("energy")
    live = block * 2 // 3
    padded = -(-live // (owners * 8)) * 8
    while energies * padded % 16:
        padded += 8
    tables = transform_tables(owners * energies, padded)
    chunk = energies * padded
    flat = owners * chunk
    slots = owners * padded
    anywhere = pl.BlockSpec(memory_space=pl.ANY)
    vmem = pl.BlockSpec(memory_space=pltpu.VMEM)
    dma = pltpu.SemaphoreType.DMA
    blocks = (2, owners, chunk, width)
    back, places = pl.pallas_call(
        functools.partial(kernel, live, padded),
        out_shape=(
            jax.ShapeDtypeStruct(blocks, BF16),
            jax.ShapeDtypeStruct((energies, block, flat), BF16),
        ),
        in_specs=[anywhere] * 5,
        out_specs=(vmem, vmem),
        scratch_shapes=[
            pltpu.VMEM(retarded.shape, BF16),
            pltpu.VMEM(injection.shape, BF16),
            pltpu.VMEM(screened.shape, BF16),
            pltpu.VMEM((1, block), pattern.dtype),
            pltpu.VMEM(tables.shape, BF16),
            pltpu.VMEM((2, 2, energies, block, width), BF16),
            pltpu.VMEM((3, energies, 2 * block, width), BF16),
            pltpu.VMEM((3, energies, slots, width), BF16),
            pltpu.VMEM((2, energies, slots, width), F32),
            pltpu.VMEM((2, flat, width), F32),
            pltpu.VMEM((owners, 2, chunk, width), BF16),
            pltpu.VMEM((owners, 2, chunk, width), BF16),
            pltpu.VMEM((2, energies, owners, padded, width), BF16),
            pltpu.VMEM((2, energies, owners, padded, width), BF16),
            pltpu.VMEM(blocks, BF16),
            dma((5,)),
            dma((2, 2, energies)),
            dma((2, 2, energies)),
            dma,
            dma,
            dma((2, energies)),
            dma((2, energies)),
            dma((2,)),
            dma((2,)),
            dma((2,)),
        ],
        compiler_params=pltpu.CompilerParams(
            collective_id=0, has_side_effects=True, vmem_limit_bytes=53 * 1024 * 1024
        ),
    )(
        retarded,
        injection,
        screened,
        pattern.reshape(1, -1),
        jnp.asarray(tables),
    )
    return pl.pallas_call(
        expand,
        out_shape=jax.ShapeDtypeStruct(screened.shape, BF16),
        in_specs=[vmem, vmem],
        out_specs=vmem,
        compiler_params=pltpu.CompilerParams(vmem_limit_bytes=32 * 1024 * 1024),
    )(back, places)


def solution(mesh):
    placed = (
        P("energy", None, "slab", None),
        P("energy", None, "slab", None),
        P("energy", None, "slab", None),
        P("slab"),
    )
    return jax.shard_map(
        local,
        mesh=mesh,
        in_specs=placed,
        out_specs=P("energy", None, "slab", None),
        check_vma=False,
    )
```
